512 devices in a mesh: dp: 128 (over z_lo, y, x, core), mp: 4 (over z_hi).
Axes of the slice: x: 4, y: 8, z: 8 (z_hi: 4, z_lo: 2; z = z_hi * 2 + z_lo), core: 2. Of those that a mesh axis runs over, the one named last changes fastest.
Arguments:
- tokens: bfloat16 [4096, 4096], P('mp'), may hold values from -6 to 6
- gate_pre: bfloat16 [4096, 16384], P('mp', 'dp'), may hold values from -8 to 8
- up_value: bfloat16 [4096, 16384], P('mp', 'dp'), may hold values from -6 to 6
- grad_hidden: bfloat16 [4096, 16384], P('mp', 'dp'), may hold values from -6 to 6
- gate_weight: bfloat16 [4096, 16384], P('mp', 'dp'), may hold values from -0.1875 to 0.1875
Outputs:
- grad_tokens: bfloat16 [4096, 4096], P('mp', 'dp')
- grad_gate_weight: bfloat16 [4096, 16384], P('mp', 'dp')
The draws below stay inside these ranges and needn't reach their ends.
All inputs are finite; a program needn't handle non-finite values.
Results may differ from the reference program's by a relative error of at most 0.0049.
Values may be sent and summed in bfloat16 or wider, within the bound.
No kernel may reach another device: no remote copies, remote signals or barrier semaphores. Data moves between devices by JAX's collectives and lax.ppermute only.
A program may use at most 128 MiB of HBM per device.

```python
import jax
import jax.numpy as jnp

D = 4096
FF = 16384
TOKENS = 4096


def with_spikes(array, rng, source, target, shards_of, factor):
    def block_of(axis_at):
        return (jnp.arange(array.shape[axis_at]) // (array.shape[axis_at] // shards_of)).reshape((-1,) + (1,) * (array.ndim - 1 - axis_at))

    near = jax.random.permutation(rng, shards_of)[block_of(target)]
    second = (block_of(target) + shards_of // 2) % shards_of
    return jnp.where((block_of(source) == near) | (block_of(source) == second), factor * array, array)


def steps_of(key, extent, split, low, high):
    loudness = 1.0
    for axis_at, shards_of in split:
        draws = jax.random.uniform(jax.random.fold_in(jax.random.fold_in(key, 6), axis_at), (shards_of,), jnp.float32, low / len(split), high / len(split))
        loudness = loudness * jnp.repeat(jnp.exp(draws), extent[axis_at] // shards_of).reshape((-1,) + (1,) * (len(extent) - 1 - axis_at))
    return loudness


def bell_draw(rng, dims, deviation, limit, shards=(), kind=jnp.bfloat16):
    gain = steps_of(rng, dims, shards, -0.22, 0.18) if shards else 1.0
    drawn = jax.random.normal(rng, dims, jnp.float32) * deviation * gain
    return jnp.minimum(jnp.maximum(drawn, -limit), limit).astype(kind)


def heavy_noise(own_key, extent, spread, reach, pieces, heavy, kind=jnp.bfloat16):
    array = spread * jax.random.normal(own_key, extent, jnp.float32)
    if pieces:
        array = array * steps_of(own_key, extent, pieces, -0.22, 0.18)
    return jnp.clip(with_spikes(array, jax.random.fold_in(own_key, 3), *heavy), -reach, reach).astype(kind)


def setup_inputs(seed: int = 0) -> dict:
    streams_of = jax.random.split(jax.random.key(seed), 6)
    tokens = heavy_noise(streams_of[0], (TOKENS, D), 1.0, 6.0, ((0, 4),), (0, 1, 4, 2.0))
    gate_pre = bell_draw(streams_of[1], (TOKENS, FF), 1.5, 8.0, ((0, 4), (1, 128)))
    up_value = bell_draw(streams_of[2], (TOKENS, FF), 1.0, 6.0, ((0, 4), (1, 128)))
    grad_hidden = bell_draw(streams_of[3], (TOKENS, FF), 1.0, 6.0, ((0, 4), (1, 128)))
    gate_weight = heavy_noise(streams_of[4], (D, FF), FF ** -0.5, 0.1875, ((0, 4), (1, 128)), (1, 0, 128, 5.5))
    return dict(tokens=tokens, gate_pre=gate_pre, up_value=up_value, grad_hidden=grad_hidden, gate_weight=gate_weight)


def reference(tokens, gate_pre, up_value, grad_hidden, gate_weight):
    gate = gate_pre.astype(jnp.float32)
    sigma = jax.nn.sigmoid(gate)
    grad_gate = (grad_hidden.astype(jnp.float32) * up_value.astype(jnp.float32) * sigma * (1.0 + gate * (1.0 - sigma))).astype(jnp.bfloat16)
    grad_tokens = jnp.dot(grad_gate, gate_weight.T, preferred_element_type=jnp.float32).astype(jnp.bfloat16)
    weight_sum = jnp.dot(tokens.T, grad_gate, preferred_element_type=jnp.float32)
    grad_gate_weight = (weight_sum * (float(TOKENS) ** -0.5)).astype(jnp.bfloat16)
    return grad_tokens, grad_gate_weight
```

```python
import jax
import jax.numpy as jnp
from jax import lax
from jax.experimental import pallas as pl
from jax.experimental.pallas import tpu as pltpu
from jax.sharding import Mesh, PartitionSpec as P

AXES = ("zl", "y", "x", "c", "mp")
STEP = 256


def shift(array, axis, size, by):
    return lax.ppermute(array, axis, [((i + by) % size, i) for i in range(size)])


def partial_kernel(order, rows_ref, *refs):
    gates, out_ref, rows, block = refs[:8], refs[8], refs[9], refs[10]

    @pl.when(pl.program_id(0) == 0)
    def _():
        for k in range(8):
            for m in range(4):
                rows[m * 128 : (m + 1) * 128, k * 128 : (k + 1) * 128] = rows_ref[m, order[k]]

    for k in range(8):
        block[:, k * 128 : (k + 1) * 128] = gates[k][...]
    out_ref[...] = lax.dot_general(
        rows[...], block[...], (((1,), (1,)), ((), ())), preferred_element_type=jnp.float32
    ).astype(jnp.bfloat16)


def partial_product(order, rows, gates):
    return pl.pallas_call(
        partial_kernel,
        grid_spec=pltpu.PrefetchScalarGridSpec(
            num_scalar_prefetch=1,
            grid=(1024 // STEP,),
            in_specs=[pl.BlockSpec((4, 8, 128, 128), lambda t, order: (0, 0, 0, 0))]
            + [pl.BlockSpec((STEP, 128), lambda t, order: (t, 0))] * 8,
            out_specs=pl.BlockSpec((512, STEP), lambda t, order: (0, t)),
            scratch_shapes=[
                pltpu.VMEM((512, 1024), jnp.bfloat16),
                pltpu.VMEM((STEP, 1024), jnp.bfloat16),
            ],
        ),
        out_shape=jax.ShapeDtypeStruct((512, 1024), jnp.bfloat16),
        compiler_params=pltpu.CompilerParams(vmem_limit_bytes=16 << 20),
        cost_estimate=pl.CostEstimate(flops=1 << 30, bytes_accessed=4 << 20, transcendentals=0),
    )(order, rows, *gates)


def sum_kernel(pieces_ref, out_ref):
    out_ref[...] = jnp.sum(pieces_ref[...].astype(jnp.float32), axis=0).astype(jnp.bfloat16)


def sum_pieces(pieces):
    return pl.pallas_call(
        sum_kernel,
        out_shape=jax.ShapeDtypeStruct(pieces.shape[1:], jnp.bfloat16),
        in_specs=[pl.BlockSpec(memory_space=pltpu.VMEM)],
        out_specs=pl.BlockSpec(memory_space=pltpu.VMEM),
    )(pieces)


def body(tokens, gate_pre, up_value, grad_hidden, gate_weight):
    rows = gate_weight.reshape(4, 8, 32, 128).swapaxes(0, 1).reshape(1, 8, 128, 128)
    rows = jnp.broadcast_to(rows, (4, 8, 128, 128)).reshape(32, 128, 128)
    rows = lax.all_to_all(rows, ("mp", "x", "c"), 0, 0, tiled=True).reshape(4, 8, 128, 128)

    gate = gate_pre.astype(jnp.float32)
    sigma = jax.nn.sigmoid(gate)
    grad_gate = (
        grad_hidden.astype(jnp.float32)
        * up_value.astype(jnp.float32)
        * sigma
        * (1.0 + gate * (1.0 - sigma))
    ).astype(jnp.bfloat16)
    total_tokens = tokens.shape[0] * lax.axis_size("mp")
    norm_factor = float(total_tokens) ** (-0.5)

    mine = [grad_gate] + [shift(grad_gate, "x", 4, k) for k in (1, 3, 2)]
    other = [shift(block, "c", 2, 1) for block in mine]
    x, c = lax.axis_index("x"), lax.axis_index("c")
    order = jnp.stack(
        [((x + k) & 3) * 2 + c for k in (0, 1, 3, 2)] + [((x + k) & 3) * 2 + 1 - c for k in (0, 1, 3, 2)]
    ).astype(jnp.int32)
    partial_sums = partial_product(order, rows, mine + other)
    pieces = lax.all_to_all(partial_sums.reshape(16, 32, 1024), ("zl", "y"), 0, 0, tiled=True)
    grad_tokens = sum_pieces(pieces).T

    share = lax.dot_general(
        grad_gate, tokens, (((0,), (0,)), ((), ())), preferred_element_type=jnp.float32
    )
    m = lax.axis_index("mp")
    summed = lax.dynamic_slice_in_dim(share, m * 1024, 1024, axis=1)
    for k in (1, 3, 2):
        away = lax.dynamic_slice_in_dim(share, ((m + k) & 3) * 1024, 1024, axis=1).astype(jnp.bfloat16)
        summed = summed + shift(away, "mp", 4, -k).astype(jnp.float32)
    grad_gate_weight = (summed * norm_factor).astype(jnp.bfloat16).T
    return (grad_tokens, grad_gate_weight)


def solution(mesh):
    fine = Mesh(mesh.devices.reshape(2, 8, 4, 2, 4), AXES)
    dp = ("zl", "y", "x", "c")
    in_specs = (P("mp", None), P("mp", dp), P("mp", dp), P("mp", dp), P("mp", dp))
    out_specs = (P("mp", dp), P("mp", dp))
    return jax.shard_map(body, mesh=fine, in_specs=in_specs, out_specs=out_specs, check_vma=False)
```

```python
import functools

import jax
import jax.numpy as jnp
from jax import lax
from jax.experimental import pallas as pl
from jax.experimental.pallas import tpu as pltpu
from jax.sharding import Mesh, PartitionSpec as P

AXES = ("zl", "y", "x", "c", "mp")
TURNS = (1, 3, 2)
BF16, F32 = jnp.bfloat16, jnp.float32
IN_HBM = pl.BlockSpec(memory_space=pltpu.HBM)
IN_VMEM = pl.BlockSpec(memory_space=pltpu.VMEM)


def shift(array, axis, size, by):
    return lax.ppermute(array, axis, [((i + by) % size, i) for i in range(size)])


def params(limit=24):
    return pltpu.CompilerParams(vmem_limit_bytes=limit << 20)


def whole(shape):
    return pl.BlockSpec(shape, lambda *_: (0,) * len(shape))


def spread_kernel(weight_ref, out_ref, weight, sem):
    copy = pltpu.make_async_copy(weight_ref, weight, sem)
    copy.start()
    copy.wait()
    for k in range(8):
        for q in range(4):
            piece = weight[(q * 8 + k) * 32 : (q * 8 + k + 1) * 32, :]
            for m in range(4):
                out_ref[m, k, q * 32 : (q + 1) * 32, :] = piece


def spread_rows(weight):
    return pl.pallas_call(
        spread_kernel,
        in_specs=[IN_HBM],
        out_specs=IN_VMEM,
        scratch_shapes=[pltpu.VMEM((1024, 128), BF16), pltpu.SemaphoreType.DMA],
        out_shape=jax.ShapeDtypeStruct((4, 8, 128, 128), BF16),
        compiler_params=params(58),
    )(weight)


def gate_kernel(gate_hbm, up_hbm, hidden_hbm, out_ref, *scratch):
    sems = scratch[3]
    copies = []
    for step in range(4):
        rows = pl.ds(step * 256, 256)
        for n, source in enumerate((gate_hbm, up_hbm, hidden_hbm)):
            copy = pltpu.make_async_copy(source.at[rows], scratch[n].at[rows], sems.at[n, step])
            copy.start()
            copies.append(copy)
    for step in range(4):
        rows = pl.ds(step * 256, 256)
        for copy in copies[step * 3 : step * 3 + 3]:
            copy.wait()
        gate, up, hidden = (ref[rows].astype(F32) for ref in scratch[:3])
        sigma = jax.nn.sigmoid(gate)
        product = hidden * up * sigma * (1.0 + gate * (1.0 - sigma))
        out_ref[:, rows] = product.T.astype(BF16)


def gate_gradient(gate_pre, up_value, grad_hidden):
    return pl.pallas_call(
        gate_kernel,
        in_specs=[IN_HBM] * 3,
        out_specs=IN_VMEM,
        scratch_shapes=[pltpu.VMEM((1024, 128), BF16)] * 3 + [pltpu.SemaphoreType.DMA((3, 4))],
        out_shape=jax.ShapeDtypeStruct((128, 1024), BF16),
        compiler_params=params(58),
    )(gate_pre, up_value, grad_hidden)


def share_kernel(gates_ref, tokens_hbm, own_ref, a_ref, b_ref, c_ref, tokens, sems):
    m = lax.axis_index("mp")
    copies = []
    for step in range(8):
        column = jnp.bitwise_and(m + (TURNS + (0,))[step // 2], 3) * 1024 + step % 2 * 512
        copy = pltpu.make_async_copy(
            tokens_hbm.at[:, pl.ds(pl.multiple_of(column, 512), 512)], tokens.at[step], sems.at[step]
        )
        copy.start()
        copies.append(copy)
    for step, copy in enumerate(copies):
        copy.wait()
        out_ref = (a_ref, b_ref, c_ref, own_ref)[step // 2]
        share = jnp.dot(gates_ref[...], tokens[step], preferred_element_type=F32)
        out_ref[:, step % 2 * 512 : (step % 2 + 1) * 512] = share.astype(out_ref.dtype)


def weight_shares(gates, tokens):
    return pl.pallas_call(
        share_kernel,
        in_specs=[IN_VMEM, IN_HBM],
        out_specs=[IN_VMEM] * 4,
        scratch_shapes=[pltpu.VMEM((8, 1024, 512), BF16), pltpu.SemaphoreType.DMA((8,))],
        out_shape=[jax.ShapeDtypeStruct((128, 1024), F32)]
        + [jax.ShapeDtypeStruct((128, 1024), BF16)] * 3,
        compiler_params=params(58),
        cost_estimate=pl.CostEstimate(flops=1 << 30, bytes_accessed=10 << 20, transcendentals=0),
    )(gates, tokens)


def add_kernel(scale, own_ref, *refs):
    total = own_ref[...]
    for ref in refs[:3]:
        total = total + ref[...].astype(F32)
    refs[3][...] = (total * scale).T.astype(BF16)


def add_shares(own, away, scale):
    return pl.pallas_call(
        functools.partial(add_kernel, scale),
        grid=(4,),
        in_specs=[pl.BlockSpec((128, 256), lambda d: (0, d))] * 4,
        out_specs=pl.BlockSpec((256, 128), lambda d: (d, 0)),
        out_shape=jax.ShapeDtypeStruct((1024, 128), BF16),
        compiler_params=params(),
    )(own, *away)


def partial_kernel(order, rows_ref, *refs):
    gates, out_ref, rows, block = refs[:8], refs[8], refs[9], refs[10]
    for k in range(8):
        for m in range(4):
            rows[m * 128 : (m + 1) * 128, k * 128 : (k + 1) * 128] = rows_ref[m, order[k]]
        block[k * 128 : (k + 1) * 128, :] = gates[k][...]
    out_ref[...] = jnp.dot(rows[...], block[...], preferred_element_type=F32).astype(BF16)


def partial_product(order, rows, gates):
    return pl.pallas_call(
        partial_kernel,
        grid_spec=pltpu.PrefetchScalarGridSpec(
            num_scalar_prefetch=1,
            grid=(1,),
            in_specs=[whole((4, 8, 128, 128))] + [whole((128, 1024))] * 8,
            out_specs=whole((512, 1024)),
            scratch_shapes=[pltpu.VMEM((512, 1024), BF16), pltpu.VMEM((1024, 1024), BF16)],
        ),
        out_shape=jax.ShapeDtypeStruct((512, 1024), BF16),
        compiler_params=params(),
        cost_estimate=pl.CostEstimate(flops=1 << 30, bytes_accessed=4 << 20, transcendentals=0),
    )(order, rows, *gates)


def sum_kernel(pieces_ref, out_ref):
    out_ref[...] = jnp.sum(pieces_ref[...].astype(F32), axis=0).astype(BF16)


def sum_pieces(pieces):
    return pl.pallas_call(
        sum_kernel,
        grid=(4,),
        in_specs=[pl.BlockSpec((16, 32, 256), lambda t: (0, 0, t))],
        out_specs=pl.BlockSpec((32, 256), lambda t: (0, t)),
        out_shape=jax.ShapeDtypeStruct((32, 1024), BF16),
        compiler_params=params(),
    )(pieces)


def body(tokens, gate_pre, up_value, grad_hidden, gate_weight):
    x, c = lax.axis_index("x"), lax.axis_index("c")
    norm_factor = float(tokens.shape[0] * lax.axis_size("mp")) ** (-0.5)

    gates = gate_gradient(gate_pre, up_value, grad_hidden)
    mine = [gates] + [shift(gates, "x", 4, k) for k in TURNS]
    other = [shift(block, "c", 2, 1) for block in mine]

    rows = spread_rows(gate_weight).reshape(32, 128, 128)
    rows = lax.all_to_all(rows, ("mp", "x", "c"), 0, 0, tiled=True).reshape(4, 8, 128, 128)

    own, *shares = weight_shares(gates, tokens)
    away = [shift(share, "mp", 4, -k) for k, share in zip(TURNS, shares)]

    order = jnp.stack(
        [((x + k) & 3) * 2 + c for k in (0,) + TURNS]
        + [((x + k) & 3) * 2 + 1 - c for k in (0,) + TURNS]
    ).astype(jnp.int32)
    order, away[0] = lax.optimization_barrier((order, away[0]))
    partial_sums = partial_product(order, rows, mine + other)
    pieces = lax.all_to_all(partial_sums.reshape(16, 32, 1024), ("zl", "y"), 0, 0, tiled=True)
    grad_tokens = sum_pieces(pieces).T
    grad_gate_weight = add_shares(own, away, norm_factor)
    return (grad_tokens, grad_gate_weight)


def solution(mesh):
    fine = Mesh(mesh.devices.reshape(2, 8, 4, 2, 4), AXES)
    dp = ("zl", "y", "x", "c")
    in_specs = (P("mp", None), P("mp", dp), P("mp", dp), P("mp", dp), P("mp", dp))
    out_specs = (P("mp", dp), P("mp", dp))
    return jax.shard_map(body, mesh=fine, in_specs=in_specs, out_specs=out_specs, check_vma=False)
```

```python
import functools

import jax
import jax.numpy as jnp
from jax import lax
from jax.experimental import pallas as pl
from jax.experimental.pallas import tpu as pltpu
from jax.sharding import Mesh, PartitionSpec as P

AXES = ("zl", "y", "x", "c", "mp")
TURNS = (1, 3, 2)
BF16, F32 = jnp.bfloat16, jnp.float32
IN_HBM = pl.BlockSpec(memory_space=pltpu.HBM)
IN_VMEM = pl.BlockSpec(memory_space=pltpu.VMEM)


def shift(array, axis, size, by):
    return lax.ppermute(array, axis, [((i + by) % size, i) for i in range(size)])


def params(limit=24):
    return pltpu.CompilerParams(vmem_limit_bytes=limit << 20)


def whole(shape):
    return pl.BlockSpec(shape, lambda *_: (0,) * len(shape))


def spread_kernel(weight_ref, out_ref, weight, sem):
    copy = pltpu.make_async_copy(weight_ref, weight, sem)
    copy.start()
    copy.wait()
    for k in range(8):
        for q in range(4):
            piece = weight[(q * 8 + k) * 32 : (q * 8 + k + 1) * 32, :]
            for m in range(4):
                out_ref[m, k, q * 32 : (q + 1) * 32, :] = piece


def spread_rows(weight):
    return pl.pallas_call(
        spread_kernel,
        in_specs=[IN_HBM],
        out_specs=IN_VMEM,
        scratch_shapes=[pltpu.VMEM((1024, 128), BF16), pltpu.SemaphoreType.DMA],
        out_shape=jax.ShapeDtypeStruct((4, 8, 128, 128), BF16),
        compiler_params=params(58),
    )(weight)


def gate_kernel(gate_hbm, up_hbm, hidden_hbm, out_ref, *scratch):
    sems = scratch[3]
    copies = []
    for step in range(4):
        rows = pl.ds(step * 256, 256)
        for n, source in enumerate((gate_hbm, up_hbm, hidden_hbm)):
            copy = pltpu.make_async_copy(source.at[rows], scratch[n].at[rows], sems.at[n, step])
            copy.start()
            copies.append(copy)
    for step in range(4):
        rows = pl.ds(step * 256, 256)
        for copy in copies[step * 3 : step * 3 + 3]:
            copy.wait()
        gate, up, hidden = (ref[rows].astype(F32) for ref in scratch[:3])
        sigma = jax.nn.sigmoid(gate)
        product = hidden * up * sigma * (1.0 + gate * (1.0 - sigma))
        out_ref[:, rows] = product.T.astype(BF16)


def gate_gradient(gate_pre, up_value, grad_hidden):
    return pl.pallas_call(
        gate_kernel,
        in_specs=[IN_HBM] * 3,
        out_specs=IN_VMEM,
        scratch_shapes=[pltpu.VMEM((1024, 128), BF16)] * 3 + [pltpu.SemaphoreType.DMA((3, 4))],
        out_shape=jax.ShapeDtypeStruct((128, 1024), BF16),
        compiler_params=params(58),
    )(gate_pre, up_value, grad_hidden)


def share_kernel(gates_ref, tokens_hbm, own_ref, right_ref, left_ref, far_a_ref, far_b_ref, tokens, sems):
    m = lax.axis_index("mp")
    turns = (2, 1, 3, 0)
    copies = []
    for step in range(8):
        column = jnp.bitwise_and(m + turns[step // 2], 3) * 1024 + step % 2 * 512
        copy = pltpu.make_async_copy(
            tokens_hbm.at[:, pl.ds(pl.multiple_of(column, 512), 512)], tokens.at[step], sems.at[step]
        )
        copy.start()
        copies.append(copy)
    for step, copy in enumerate(copies):
        copy.wait()
        columns = pl.ds(step % 2 * 512, 512)
        share = jnp.dot(gates_ref[...], tokens[step], preferred_element_type=F32)
        if step < 2:
            far_a_ref[:, columns] = share[:64].astype(BF16)
            far_b_ref[:, columns] = share[64:].astype(BF16)
        else:
            (right_ref, left_ref, own_ref)[step // 2 - 1][:, columns] = share


def weight_shares(gates, tokens):
    full, half = jax.ShapeDtypeStruct((128, 1024), F32), jax.ShapeDtypeStruct((64, 1024), BF16)
    return pl.pallas_call(
        share_kernel,
        in_specs=[IN_VMEM, IN_HBM],
        out_specs=[IN_VMEM] * 5,
        scratch_shapes=[pltpu.VMEM((8, 1024, 512), BF16), pltpu.SemaphoreType.DMA((8,))],
        out_shape=[full, full, full, half, half],
        compiler_params=params(55),
        cost_estimate=pl.CostEstimate(flops=1 << 30, bytes_accessed=10 << 20, transcendentals=0),
    )(gates, tokens)


def relay_kernel(right_ref, left_ref, far_a_ref, far_b_ref, right_out, left_out):
    right_out[:64] = (right_ref[:64] + far_a_ref[...].astype(F32)).astype(BF16)
    right_out[64:] = right_ref[64:].astype(BF16)
    left_out[:64] = left_ref[:64].astype(BF16)
    left_out[64:] = (left_ref[64:] + far_b_ref[...].astype(F32)).astype(BF16)


def relay_shares(right, left, far_a, far_b):
    return pl.pallas_call(
        relay_kernel,
        grid=(4,),
        in_specs=[pl.BlockSpec((128, 256), lambda d: (0, d))] * 2
        + [pl.BlockSpec((64, 256), lambda d: (0, d))] * 2,
        out_specs=[pl.BlockSpec((128, 256), lambda d: (0, d))] * 2,
        out_shape=[jax.ShapeDtypeStruct((128, 1024), BF16)] * 2,
        compiler_params=params(),
    )(right, left, far_a, far_b)


def add_kernel(scale, own_ref, *refs):
    total = own_ref[...]
    for ref in refs[:2]:
        total = total + ref[...].astype(F32)
    refs[2][...] = (total * scale).T.astype(BF16)


def add_shares(own, away, scale):
    return pl.pallas_call(
        functools.partial(add_kernel, scale),
        grid=(4,),
        in_specs=[pl.BlockSpec((128, 256), lambda d: (0, d))] * 3,
        out_specs=pl.BlockSpec((256, 128), lambda d: (d, 0)),
        out_shape=jax.ShapeDtypeStruct((1024, 128), BF16),
        compiler_params=params(),
    )(own, *away)


def partial_kernel(order, rows_ref, mine_ref, other_ref, out_ref, rows):
    for k in range(8):
        for m in range(4):
            rows[m * 128 : (m + 1) * 128, k * 128 : (k + 1) * 128] = rows_ref[m, order[k]]
    total = jnp.dot(rows[:, :512], mine_ref[...].reshape(512, 1024), preferred_element_type=F32)
    total += jnp.dot(rows[:, 512:], other_ref[...].reshape(512, 1024), preferred_element_type=F32)
    out_ref[...] = total.astype(BF16)


def partial_product(order, rows, mine, other):
    return pl.pallas_call(
        partial_kernel,
        grid_spec=pltpu.PrefetchScalarGridSpec(
            num_scalar_prefetch=1,
            grid=(1,),
            in_specs=[whole((4, 8, 128, 128))] + [whole((4, 128, 1024))] * 2,
            out_specs=whole((512, 1024)),
            scratch_shapes=[pltpu.VMEM((512, 1024), BF16)],
        ),
        out_shape=jax.ShapeDtypeStruct((512, 1024), BF16),
        compiler_params=params(),
        cost_estimate=pl.CostEstimate(flops=1 << 30, bytes_accessed=4 << 20, transcendentals=0),
    )(order, rows, mine, other)


def sum_kernel(pieces_ref, out_ref):
    out_ref[...] = jnp.sum(pieces_ref[...].astype(F32), axis=0).astype(BF16)


def sum_pieces(pieces):
    return pl.pallas_call(
        sum_kernel,
        grid=(4,),
        in_specs=[pl.BlockSpec((16, 32, 256), lambda t: (0, 0, t))],
        out_specs=pl.BlockSpec((32, 256), lambda t: (0, t)),
        out_shape=jax.ShapeDtypeStruct((32, 1024), BF16),
        compiler_params=params(),
    )(pieces)


def body(tokens, gate_pre, up_value, grad_hidden, gate_weight):
    x, c = lax.axis_index("x"), lax.axis_index("c")
    norm_factor = float(tokens.shape[0] * lax.axis_size("mp")) ** (-0.5)

    gates = gate_gradient(gate_pre, up_value, grad_hidden)
    weight, gates = lax.optimization_barrier((gate_weight, gates))
    rows = spread_rows(weight).reshape(32, 128, 128)
    rows = lax.all_to_all(rows, ("mp", "x", "c"), 0, 0, tiled=True).reshape(4, 8, 128, 128)

    mine = [shift(gates, "x", 4, k) for k in TURNS]
    own, right, left, far_a, far_b = weight_shares(gates, tokens)
    *mine, own = lax.optimization_barrier((*mine, own))
    far_a, far_b = shift(far_a, "mp", 4, -1), shift(far_b, "mp", 4, 1)
    mine = jnp.stack([gates, *mine])
    other = shift(mine, "c", 2, 1)

    order = jnp.stack(
        [((x + k) & 3) * 2 + c for k in (0,) + TURNS]
        + [((x + k) & 3) * 2 + 1 - c for k in (0,) + TURNS]
    ).astype(jnp.int32)
    partial_sums = partial_product(order, rows, mine, other)
    partial_sums, far_a, far_b = lax.optimization_barrier((partial_sums, far_a, far_b))
    pieces = lax.all_to_all(partial_sums.reshape(16, 32, 1024), ("zl", "y"), 0, 0, tiled=True)

    right, left = relay_shares(right, left, far_a, far_b)
    away = shift(right, "mp", 4, -1), shift(left, "mp", 4, 1)
    grad_gate_weight = add_shares(own, away, norm_factor)
    grad_tokens = sum_pieces(pieces).T
    return (grad_tokens, grad_gate_weight)


def solution(mesh):
    fine = Mesh(mesh.devices.reshape(2, 8, 4, 2, 4), AXES)
    dp = ("zl", "y", "x", "c")
    in_specs = (P("mp", None), P("mp", dp), P("mp", dp), P("mp", dp), P("mp", dp))
    out_specs = (P("mp", dp), P("mp", dp))
    return jax.shard_map(body, mesh=fine, in_specs=in_specs, out_specs=out_specs, check_vma=False)
```

```python
import functools

import jax
import jax.numpy as jnp
from jax import lax
from jax.experimental import pallas as pl
from jax.experimental.pallas import tpu as pltpu
from jax.sharding import Mesh, PartitionSpec as P

AXES = ("zl", "y", "x", "c", "mp")
TURNS = (1, 3, 2)
BF16, F32 = jnp.bfloat16, jnp.float32
IN_HBM = pl.BlockSpec(memory_space=pltpu.HBM)
IN_VMEM = pl.BlockSpec(memory_space=pltpu.VMEM)


def shift(array, axis, size, by):
    return lax.ppermute(array, axis, [((i + by) % size, i) for i in range(size)])


def params(limit=24):
    return pltpu.CompilerParams(vmem_limit_bytes=limit << 20)


def whole(shape):
    return pl.BlockSpec(shape, lambda *_: (0,) * len(shape))


def spread_kernel(weight_ref, out_ref, weight, sem):
    copy = pltpu.make_async_copy(weight_ref, weight, sem)
    copy.start()
    copy.wait()
    for k in range(8):
        for q in range(4):
            piece = weight[(q * 8 + k) * 32 : (q * 8 + k + 1) * 32, :]
            for m in range(4):
                out_ref[m, k, q * 32 : (q + 1) * 32, :] = piece


def spread_rows(weight):
    return pl.pallas_call(
        spread_kernel,
        in_specs=[IN_HBM],
        out_specs=IN_VMEM,
        scratch_shapes=[pltpu.VMEM((1024, 128), BF16), pltpu.SemaphoreType.DMA],
        out_shape=jax.ShapeDtypeStruct((4, 8, 128, 128), BF16),
        compiler_params=params(58),
    )(weight)


def gate_kernel(gate_hbm, up_hbm, hidden_hbm, out_ref, *scratch):
    sems = scratch[3]
    copies = []
    for step in range(4):
        rows = pl.ds(step * 256, 256)
        for n, source in enumerate((gate_hbm, up_hbm, hidden_hbm)):
            copy = pltpu.make_async_copy(source.at[rows], scratch[n].at[rows], sems.at[n, step])
            copy.start()
            copies.append(copy)
    for step in range(4):
        rows = pl.ds(step * 256, 256)
        for copy in copies[step * 3 : step * 3 + 3]:
            copy.wait()
        gate, up, hidden = (ref[rows].astype(F32) for ref in scratch[:3])
        sigma = jax.nn.sigmoid(gate)
        product = hidden * up * sigma * (1.0 + gate * (1.0 - sigma))
        out_ref[:, rows] = product.T.astype(BF16)


def gate_gradient(gate_pre, up_value, grad_hidden):
    return pl.pallas_call(
        gate_kernel,
        in_specs=[IN_HBM] * 3,
        out_specs=IN_VMEM,
        scratch_shapes=[pltpu.VMEM((1024, 128), BF16)] * 3 + [pltpu.SemaphoreType.DMA((3, 4))],
        out_shape=jax.ShapeDtypeStruct((128, 1024), BF16),
        compiler_params=params(58),
    )(gate_pre, up_value, grad_hidden)


def share_kernel(gates_ref, tokens_hbm, own_ref, a_ref, b_ref, c_ref, tokens, sems):
    m = lax.axis_index("mp")
    copies = []
    for step in range(8):
        column = jnp.bitwise_and(m + ((2, 1, 3, 0)[step // 2]), 3) * 1024 + step % 2 * 512
        copy = pltpu.make_async_copy(
            tokens_hbm.at[:, pl.ds(pl.multiple_of(column, 512), 512)], tokens.at[step], sems.at[step]
        )
        copy.start()
        copies.append(copy)
    for step, copy in enumerate(copies):
        copy.wait()
        out_ref = (c_ref, a_ref, b_ref, own_ref)[step // 2]
        share = jnp.dot(gates_ref[...], tokens[step], preferred_element_type=F32)
        out_ref[:, step % 2 * 512 : (step % 2 + 1) * 512] = share.astype(out_ref.dtype)


def weight_shares(gates, tokens):
    return pl.pallas_call(
        share_kernel,
        in_specs=[IN_VMEM, IN_HBM],
        out_specs=[IN_VMEM] * 4,
        scratch_shapes=[pltpu.VMEM((8, 1024, 512), BF16), pltpu.SemaphoreType.DMA((8,))],
        out_shape=[jax.ShapeDtypeStruct((128, 1024), F32)]
        + [jax.ShapeDtypeStruct((128, 1024), BF16)] * 3,
        compiler_params=params(58),
        cost_estimate=pl.CostEstimate(flops=1 << 30, bytes_accessed=10 << 20, transcendentals=0),
    )(gates, tokens)


def add_kernel(scale, own_ref, *refs):
    total = own_ref[...]
    for ref in refs[:3]:
        total = total + ref[...].astype(F32)
    refs[3][...] = (total * scale).T.astype(BF16)


def add_shares(own, away, scale):
    return pl.pallas_call(
        functools.partial(add_kernel, scale),
        grid=(4,),
        in_specs=[pl.BlockSpec((128, 256), lambda d: (0, d))] * 4,
        out_specs=pl.BlockSpec((256, 128), lambda d: (d, 0)),
        out_shape=jax.ShapeDtypeStruct((1024, 128), BF16),
        compiler_params=params(),
    )(own, *away)


def partial_kernel(order, rows_ref, mine_ref, other_ref, out_ref, rows):
    for k in range(8):
        for m in range(4):
            rows[m * 128 : (m + 1) * 128, k * 128 : (k + 1) * 128] = rows_ref[m, order[k]]
    total = jnp.dot(rows[:, :512], mine_ref[...].reshape(512, 1024), preferred_element_type=F32)
    total += jnp.dot(rows[:, 512:], other_ref[...].reshape(512, 1024), preferred_element_type=F32)
    out_ref[...] = total.astype(BF16)


def partial_product(order, rows, mine, other):
    return pl.pallas_call(
        partial_kernel,
        grid_spec=pltpu.PrefetchScalarGridSpec(
            num_scalar_prefetch=1,
            grid=(1,),
            in_specs=[whole((4, 8, 128, 128))] + [whole((4, 128, 1024))] * 2,
            out_specs=whole((512, 1024)),
            scratch_shapes=[pltpu.VMEM((512, 1024), BF16)],
        ),
        out_shape=jax.ShapeDtypeStruct((512, 1024), BF16),
        compiler_params=params(),
        cost_estimate=pl.CostEstimate(flops=1 << 30, bytes_accessed=4 << 20, transcendentals=0),
    )(order, rows, mine, other)


def sum_kernel(pieces_ref, out_ref):
    out_ref[...] = jnp.sum(pieces_ref[...].astype(F32), axis=0).astype(BF16)


def sum_pieces(pieces):
    return pl.pallas_call(
        sum_kernel,
        grid=(4,),
        in_specs=[pl.BlockSpec((16, 32, 256), lambda t: (0, 0, t))],
        out_specs=pl.BlockSpec((32, 256), lambda t: (0, t)),
        out_shape=jax.ShapeDtypeStruct((32, 1024), BF16),
        compiler_params=params(),
    )(pieces)


def body(tokens, gate_pre, up_value, grad_hidden, gate_weight):
    x, c = lax.axis_index("x"), lax.axis_index("c")
    norm_factor = float(tokens.shape[0] * lax.axis_size("mp")) ** (-0.5)

    rows = spread_rows(gate_weight).reshape(32, 128, 128)
    rows = lax.all_to_all(rows, ("mp", "x", "c"), 0, 0, tiled=True).reshape(4, 8, 128, 128)

    gates = gate_gradient(gate_pre, up_value, grad_hidden)
    mine = [shift(gates, "x", 4, k) for k in TURNS]
    own, *shares = weight_shares(gates, tokens)
    *mine, own = lax.optimization_barrier((*mine, own))
    away = [shift(share, "mp", 4, -k) for k, share in zip(TURNS, shares)]
    mine = jnp.stack([gates, *mine])
    other = shift(mine, "c", 2, 1)

    order = jnp.stack(
        [((x + k) & 3) * 2 + c for k in (0,) + TURNS]
        + [((x + k) & 3) * 2 + 1 - c for k in (0,) + TURNS]
    ).astype(jnp.int32)

    def exchange(order, rows, mine, other):
        partial_sums = partial_product(order, rows, mine, other)
        pieces = lax.all_to_all(partial_sums.reshape(16, 32, 1024), ("zl", "y"), 0, 0, tiled=True)
        return sum_pieces(pieces)

    def never(order, rows, mine, other):
        return jnp.zeros((32, 1024), BF16)

    grad_tokens = lax.cond(order[0] >= 0, exchange, never, order, rows, mine, other)
    grad_tokens, own, *away = lax.optimization_barrier((grad_tokens, own, *away))
    grad_gate_weight = add_shares(own, away, norm_factor)
    return (grad_tokens.T, grad_gate_weight)


def solution(mesh):
    fine = Mesh(mesh.devices.reshape(2, 8, 4, 2, 4), AXES)
    dp = ("zl", "y", "x", "c")
    in_specs = (P("mp", None), P("mp", dp), P("mp", dp), P("mp", dp), P("mp", dp))
    out_specs = (P("mp", dp), P("mp", dp))
    return jax.shard_map(body, mesh=fine, in_specs=in_specs, out_specs=out_specs, check_vma=False)
```

```python
import functools

import jax
import jax.numpy as jnp
from jax import lax
from jax.experimental import pallas as pl
from jax.experimental.pallas import tpu as pltpu
from jax.sharding import Mesh, PartitionSpec as P

TURNS = (1, 3, 2)
AXES = ("zl", "y", "x", "c", "mp")
BF16, F32 = jnp.bfloat16, jnp.float32
IN_HBM = pl.BlockSpec(memory_space=pltpu.HBM)
IN_VMEM = pl.BlockSpec(memory_space=pltpu.VMEM)


def shift(array, axis, size, by):
    return lax.ppermute(array, axis, [((i + by) % size, i) for i in range(size)])


def params(limit=24):
    return pltpu.CompilerParams(vmem_limit_bytes=limit << 20)


def spread_kernel(weight_ref, out_ref, sems):
    copies = [
        pltpu.make_async_copy(weight_ref.at[:, k], out_ref.at[m, k], sems.at[m, k])
        for m in range(4)
        for k in range(8)
    ]
    for copy in copies:
        copy.start()
    for copy in copies:
        copy.wait()


def spread_rows(weight):
    return pl.pallas_call(
        spread_kernel,
        in_specs=[IN_HBM],
        out_specs=IN_HBM,
        scratch_shapes=[pltpu.SemaphoreType.DMA((4, 8))],
        out_shape=jax.ShapeDtypeStruct((4, 8, 4, 32, 128), BF16),
        compiler_params=params(58),
    )(weight.reshape(4, 8, 32, 128))


def gate_kernel(gate_hbm, up_hbm, hidden_hbm, out_ref, *scratch):
    sems = scratch[3]
    copies = []
    for step in range(4):
        rows = pl.ds(step * 256, 256)
        for n, source in enumerate((gate_hbm, up_hbm, hidden_hbm)):
            copy = pltpu.make_async_copy(source.at[rows], scratch[n].at[rows], sems.at[n, step])
            copy.start()
            copies.append(copy)
    for step in range(4):
        rows = pl.ds(step * 256, 256)
        for copy in copies[step * 3 : step * 3 + 3]:
            copy.wait()
        gate, up, hidden = (ref[rows].astype(F32) for ref in scratch[:3])
        sigma = jax.nn.sigmoid(gate)
        product = hidden * up * sigma * (1.0 + gate * (1.0 - sigma))
        out_ref[:, rows] = product.T.astype(BF16)


def gate_gradient(gate_pre, up_value, grad_hidden):
    return pl.pallas_call(
        gate_kernel,
        in_specs=[IN_HBM] * 3,
        out_specs=IN_VMEM,
        scratch_shapes=[pltpu.VMEM((1024, 128), BF16)] * 3 + [pltpu.SemaphoreType.DMA((3, 4))],
        out_shape=jax.ShapeDtypeStruct((128, 1024), BF16),
        compiler_params=params(58),
    )(gate_pre, up_value, grad_hidden)


def share_kernel(gates_ref, tokens_hbm, own_ref, right_ref, left_ref, far_ref, tokens, sems):
    m = lax.axis_index("mp")
    copies = []
    for step in range(8):
        column = jnp.bitwise_and(m + (2, 1, 3, 0)[step // 2], 3) * 1024 + step % 2 * 512
        copy = pltpu.make_async_copy(
            tokens_hbm.at[:, pl.ds(pl.multiple_of(column, 512), 512)], tokens.at[step], sems.at[step]
        )
        copy.start()
        copies.append(copy)
    for step, copy in enumerate(copies):
        copy.wait()
        out_ref = (far_ref, right_ref, left_ref, own_ref)[step // 2]
        share = jnp.dot(gates_ref[...], tokens[step], preferred_element_type=F32)
        out_ref[:, step % 2 * 512 : (step % 2 + 1) * 512] = share.astype(out_ref.dtype)


def weight_shares(gates, tokens):
    return pl.pallas_call(
        share_kernel,
        in_specs=[IN_VMEM, IN_HBM],
        out_specs=[IN_VMEM] * 4,
        scratch_shapes=[pltpu.VMEM((8, 1024, 512), BF16), pltpu.SemaphoreType.DMA((8,))],
        out_shape=[jax.ShapeDtypeStruct((128, 1024), F32)]
        + [jax.ShapeDtypeStruct((128, 1024), BF16)] * 3,
        compiler_params=params(54),
        cost_estimate=pl.CostEstimate(flops=1 << 30, bytes_accessed=10 << 20, transcendentals=0),
    )(gates, tokens)


def add_kernel(scale, own_ref, right_ref, left_ref, far_ref, out_ref):
    total = own_ref[...]
    for ref in (right_ref, left_ref, far_ref):
        total += ref[...].astype(F32)
    out_ref[...] = (total * scale).T.astype(BF16)


def add_shares(own, away, scale):
    return pl.pallas_call(
        functools.partial(add_kernel, scale),
        in_specs=[IN_VMEM] * 4,
        out_specs=IN_VMEM,
        out_shape=jax.ShapeDtypeStruct((1024, 128), BF16),
        compiler_params=params(),
    )(own, *away)


def partial_kernel(rows_ref, mine_ref, other_ref, out_ref, rows):
    x, c = lax.axis_index("x"), lax.axis_index("c")
    for k in range(8):
        turn = ((0,) + TURNS)[k % 4]
        source = jnp.bitwise_and(x + turn, 3) * 2 + (c if k < 4 else 1 - c)
        for m in range(4):
            rows[m * 128 : (m + 1) * 128, k * 128 : (k + 1) * 128] = rows_ref[m, source]
    for t in range(2):
        columns = pl.ds(t * 512, 512)
        total = jnp.dot(
            rows[:, :512], mine_ref[:, :, columns].reshape(512, 512), preferred_element_type=F32
        )
        total += jnp.dot(
            rows[:, 512:], other_ref[:, :, columns].reshape(512, 512), preferred_element_type=F32
        )
        out_ref[:, columns] = total.astype(BF16)


def partial_product(rows, mine, other):
    return pl.pallas_call(
        partial_kernel,
        in_specs=[IN_VMEM] * 3,
        out_specs=IN_VMEM,
        scratch_shapes=[pltpu.VMEM((512, 1024), BF16)],
        out_shape=jax.ShapeDtypeStruct((512, 1024), BF16),
        compiler_params=params(),
        cost_estimate=pl.CostEstimate(flops=1 << 30, bytes_accessed=4 << 20, transcendentals=0),
    )(rows, mine, other)


def sum_kernel(pieces_ref, out_ref):
    out_ref[...] = jnp.sum(pieces_ref[...].astype(F32), axis=0).astype(BF16)


def sum_pieces(pieces):
    return pl.pallas_call(
        sum_kernel,
        in_specs=[IN_VMEM],
        out_specs=IN_VMEM,
        out_shape=jax.ShapeDtypeStruct((32, 1024), BF16),
        compiler_params=params(),
    )(pieces)


def always(function, *operands):
    shapes = jax.eval_shape(function, *operands)

    def never(*_):
        return jax.tree.map(lambda shape: jnp.zeros(shape.shape, shape.dtype), shapes)

    return lax.cond(lax.axis_index("x") * 2 + lax.axis_index("c") >= 0, function, never, *operands)


def body(tokens, gate_pre, up_value, grad_hidden, gate_weight):
    norm_factor = float(tokens.shape[0] * lax.axis_size("mp")) ** (-0.5)

    rows = spread_rows(gate_weight).reshape(32, 128, 128)
    rows = lax.all_to_all(rows, ("mp", "x", "c"), 0, 0, tiled=True).reshape(4, 8, 128, 128)

    gates = gate_gradient(gate_pre, up_value, grad_hidden)
    mine = [shift(gates, "x", 4, k) for k in TURNS]
    own, *shares = weight_shares(gates, tokens)
    *mine, own = lax.optimization_barrier((*mine, own))
    away = [shift(share, "mp", 4, -k) for k, share in zip(TURNS, shares)]

    def exchange(rows, *mine):
        mine = jnp.stack(mine)
        partial_sums = partial_product(rows, mine, shift(mine, "c", 2, 1))
        pieces = lax.all_to_all(partial_sums.reshape(16, 32, 1024), ("zl", "y"), 0, 0, tiled=True)
        return sum_pieces(pieces)

    grad_tokens = always(exchange, rows, gates, *mine)
    grad_tokens, own, *away = lax.optimization_barrier((grad_tokens, own, *away))
    return (grad_tokens.T, add_shares(own, away, norm_factor))


def solution(mesh):
    fine = Mesh(mesh.devices.reshape(2, 8, 4, 2, 4), AXES)
    dp = ("zl", "y", "x", "c")
    in_specs = (P("mp", None), P("mp", dp), P("mp", dp), P("mp", dp), P("mp", dp))
    out_specs = (P("mp", dp), P("mp", dp))
    return jax.shard_map(body, mesh=fine, in_specs=in_specs, out_specs=out_specs, check_vma=False)
```

```python
import functools

import jax
import jax.numpy as jnp
from jax import lax
from jax.experimental import pallas as pl
from jax.experimental.pallas import tpu as pltpu
from jax.sharding import Mesh, PartitionSpec as P

TURNS = (1, 3, 2)
AHEAD = 3
AXES = ("zl", "y", "x", "c", "mp")
BF16, F32 = jnp.bfloat16, jnp.float32
IN_HBM = pl.BlockSpec(memory_space=pltpu.HBM)
IN_VMEM = pl.BlockSpec(memory_space=pltpu.VMEM)


def shift(array, axis, size, by):
    return lax.ppermute(array, axis, [((i + by) % size, i) for i in range(size)])


def params(limit=24):
    return pltpu.CompilerParams(vmem_limit_bytes=limit << 20)


def spread_kernel(weight_hbm, out_hbm, weight, spread, sems):
    copy = pltpu.make_async_copy(weight_hbm, weight, sems.at[4])
    copy.start()
    copy.wait()
    for k in range(8):
        for q in range(4):
            spread[k, q * 32 : (q + 1) * 32, :] = weight[(q * 8 + k) * 32 : (q * 8 + k + 1) * 32, :]
    copies = [pltpu.make_async_copy(spread, out_hbm.at[m], sems.at[m]) for m in range(4)]
    for copy in copies:
        copy.start()
    for copy in copies:
        copy.wait()


def spread_rows(weight):
    return pl.pallas_call(
        spread_kernel,
        in_specs=[IN_HBM],
        out_specs=IN_HBM,
        scratch_shapes=[
            pltpu.VMEM((1024, 128), BF16),
            pltpu.VMEM((8, 128, 128), BF16),
            pltpu.SemaphoreType.DMA((5,)),
        ],
        out_shape=jax.ShapeDtypeStruct((4, 8, 128, 128), BF16),
        compiler_params=params(58),
    )(weight)


def gate_kernel(gate_hbm, up_hbm, hidden_hbm, out_ref, *scratch):
    sems = scratch[3]
    copies = []
    for step in range(4):
        rows = pl.ds(step * 256, 256)
        for n, source in enumerate((gate_hbm, up_hbm, hidden_hbm)):
            copy = pltpu.make_async_copy(source.at[rows], scratch[n].at[rows], sems.at[n, step])
            copy.start()
            copies.append(copy)
    for step in range(4):
        rows = pl.ds(step * 256, 256)
        for copy in copies[step * 3 : step * 3 + 3]:
            copy.wait()
        gate, up, hidden = (ref[rows].astype(F32) for ref in scratch[:3])
        sigma = jax.nn.sigmoid(gate)
        product = hidden * up * sigma * (1.0 + gate * (1.0 - sigma))
        out_ref[:, rows] = product.T.astype(BF16)


def gate_gradient(gate_pre, up_value, grad_hidden):
    return pl.pallas_call(
        gate_kernel,
        in_specs=[IN_HBM] * 3,
        out_specs=IN_VMEM,
        scratch_shapes=[pltpu.VMEM((1024, 128), BF16)] * 3 + [pltpu.SemaphoreType.DMA((3, 4))],
        out_shape=jax.ShapeDtypeStruct((128, 1024), BF16),
        compiler_params=params(58),
    )(gate_pre, up_value, grad_hidden)


def share_kernel(turns, gates_ref, tokens_hbm, *refs):
    out_refs, tokens, sems = refs[: len(turns)], refs[-2], refs[-1]
    m = lax.axis_index("mp")
    copies = []
    for step in range(2 * len(turns)):
        column = jnp.bitwise_and(m + turns[step // 2], 3) * 1024 + step % 2 * 512
        copies.append(
            pltpu.make_async_copy(
                tokens_hbm.at[:, pl.ds(pl.multiple_of(column, 512), 512)], tokens.at[step], sems.at[step]
            )
        )
    for copy in copies[:AHEAD]:
        copy.start()
    for step, copy in enumerate(copies):
        copy.wait()
        if step + AHEAD < len(copies):
            copies[step + AHEAD].start()
        out_ref = out_refs[step // 2]
        share = jnp.dot(gates_ref[...], tokens[step], preferred_element_type=F32)
        out_ref[:, step % 2 * 512 : (step % 2 + 1) * 512] = share.astype(out_ref.dtype)


def weight_shares(turns, gates, tokens):
    return pl.pallas_call(
        functools.partial(share_kernel, turns),
        in_specs=[IN_VMEM, IN_HBM],
        out_specs=[IN_VMEM] * len(turns),
        scratch_shapes=[
            pltpu.VMEM((2 * len(turns), 1024, 512), BF16),
            pltpu.SemaphoreType.DMA((2 * len(turns),)),
        ],
        out_shape=[jax.ShapeDtypeStruct((128, 1024), BF16 if turn else F32) for turn in turns],
        compiler_params=params(54),
        cost_estimate=pl.CostEstimate(flops=1 << 29, bytes_accessed=5 << 20, transcendentals=0),
    )(gates, tokens)


def add_kernel(scale, own_ref, right_ref, left_ref, far_ref, out_ref):
    total = own_ref[...]
    for ref in (right_ref, left_ref, far_ref):
        total += ref[...].astype(F32)
    out_ref[...] = (total * scale).T.astype(BF16)


def add_shares(own, away, scale):
    return pl.pallas_call(
        functools.partial(add_kernel, scale),
        in_specs=[IN_VMEM] * 4,
        out_specs=IN_VMEM,
        out_shape=jax.ShapeDtypeStruct((1024, 128), BF16),
        compiler_params=params(),
    )(own, *away)


def partial_kernel(rows_ref, mine_ref, other_ref, out_ref, rows):
    x, c = lax.axis_index("x"), lax.axis_index("c")
    for k in range(8):
        turn = ((0,) + TURNS)[k % 4]
        source = jnp.bitwise_and(x + turn, 3) * 2 + (c if k < 4 else 1 - c)
        for m in range(4):
            rows[m * 128 : (m + 1) * 128, k * 128 : (k + 1) * 128] = rows_ref[m, source]
    for t in range(2):
        columns = pl.ds(t * 512, 512)
        total = jnp.dot(
            rows[:, :512], mine_ref[:, :, columns].reshape(512, 512), preferred_element_type=F32
        )
        total += jnp.dot(
            rows[:, 512:], other_ref[:, :, columns].reshape(512, 512), preferred_element_type=F32
        )
        out_ref[:, columns] = total.astype(BF16)


def partial_product(rows, mine, other):
    return pl.pallas_call(
        partial_kernel,
        in_specs=[IN_VMEM] * 3,
        out_specs=IN_VMEM,
        scratch_shapes=[pltpu.VMEM((512, 1024), BF16)],
        out_shape=jax.ShapeDtypeStruct((512, 1024), BF16),
        compiler_params=params(),
        cost_estimate=pl.CostEstimate(flops=1 << 30, bytes_accessed=4 << 20, transcendentals=0),
    )(rows, mine, other)


def sum_kernel(pieces_ref, out_ref):
    out_ref[...] = jnp.sum(pieces_ref[...].astype(F32), axis=0).astype(BF16)


def sum_pieces(pieces):
    return pl.pallas_call(
        sum_kernel,
        in_specs=[IN_VMEM],
        out_specs=IN_VMEM,
        out_shape=jax.ShapeDtypeStruct((32, 1024), BF16),
        compiler_params=params(),
    )(pieces)


def always(function, *operands):
    shapes = jax.eval_shape(function, *operands)

    def never(*_):
        return jax.tree.map(lambda shape: jnp.zeros(shape.shape, shape.dtype), shapes)

    return lax.cond(lax.axis_index("x") * 2 + lax.axis_index("c") >= 0, function, never, *operands)


def body(tokens, gate_pre, up_value, grad_hidden, gate_weight):
    norm_factor = float(tokens.shape[0] * lax.axis_size("mp")) ** (-0.5)

    rows = spread_rows(gate_weight).reshape(32, 128, 128)
    rows = lax.all_to_all(rows, ("mp", "x", "c"), 0, 0, tiled=True).reshape(4, 8, 128, 128)

    gates = gate_gradient(gate_pre, up_value, grad_hidden)
    mine = [shift(gates, "x", 4, k) for k in TURNS]
    right, left = weight_shares((1, 3), gates, tokens)
    right, left = shift(right, "mp", 4, -1), shift(left, "mp", 4, 1)

    def exchange(rows, tokens, *mine):
        gates, mine = mine[0], jnp.stack(mine)
        partial_sums = partial_product(rows, mine, shift(mine, "c", 2, 1))
        pieces = lax.all_to_all(partial_sums.reshape(16, 32, 1024), ("zl", "y"), 0, 0, tiled=True)
        far, own = weight_shares((2, 0), gates, tokens)
        return sum_pieces(pieces), own, shift(far, "mp", 4, 2)

    grad_tokens, own, far = always(exchange, rows, tokens, gates, *mine)
    grad_tokens, own, right, left, far = lax.optimization_barrier((grad_tokens, own, right, left, far))
    return (grad_tokens.T, add_shares(own, (right, left, far), norm_factor))


def solution(mesh):
    fine = Mesh(mesh.devices.reshape(2, 8, 4, 2, 4), AXES)
    dp = ("zl", "y", "x", "c")
    in_specs = (P("mp", None), P("mp", dp), P("mp", dp), P("mp", dp), P("mp", dp))
    out_specs = (P("mp", dp), P("mp", dp))
    return jax.shard_map(body, mesh=fine, in_specs=in_specs, out_specs=out_specs, check_vma=False)
```

```python
import functools

import jax
import jax.numpy as jnp
from jax import lax
from jax.experimental import pallas as pl
from jax.experimental.pallas import tpu as pltpu
from jax.sharding import Mesh, PartitionSpec as P

TURNS = (1, 3, 2)
AXES = ("zl", "y", "x", "c", "mp")
BF16, F32 = jnp.bfloat16, jnp.float32
IN_HBM = pl.BlockSpec(memory_space=pltpu.HBM)
IN_VMEM = pl.BlockSpec(memory_space=pltpu.VMEM)


def shift(array, axis, size, by):
    return lax.ppermute(array, axis, [((i + by) % size, i) for i in range(size)])


def params(limit=24):
    return pltpu.CompilerParams(vmem_limit_bytes=limit << 20)


def spread_kernel(weight_hbm, out_hbm, weight, spread, sems):
    copy = pltpu.make_async_copy(weight_hbm, weight, sems.at[4])
    copy.start()
    copy.wait()
    for k in range(8):
        for q in range(4):
            spread[k, q * 32 : (q + 1) * 32, :] = weight[(q * 8 + k) * 32 : (q * 8 + k + 1) * 32, :]
    copies = [pltpu.make_async_copy(spread, out_hbm.at[m], sems.at[m]) for m in range(4)]
    for copy in copies:
        copy.start()
    for copy in copies:
        copy.wait()


def spread_rows(weight):
    return pl.pallas_call(
        spread_kernel,
        in_specs=[IN_HBM],
        out_specs=IN_HBM,
        scratch_shapes=[
            pltpu.VMEM((1024, 128), BF16),
            pltpu.VMEM((8, 128, 128), BF16),
            pltpu.SemaphoreType.DMA((5,)),
        ],
        out_shape=jax.ShapeDtypeStruct((4, 8, 128, 128), BF16),
        compiler_params=params(58),
    )(weight)


def gate_kernel(gate_hbm, up_hbm, hidden_hbm, out_ref, *scratch):
    sems = scratch[3]
    copies = []
    for step in range(4):
        rows = pl.ds(step * 256, 256)
        for n, source in enumerate((gate_hbm, up_hbm, hidden_hbm)):
            copy = pltpu.make_async_copy(source.at[rows], scratch[n].at[rows], sems.at[n, step])
            copy.start()
            copies.append(copy)
    for step in range(4):
        rows = pl.ds(step * 256, 256)
        for copy in copies[step * 3 : step * 3 + 3]:
            copy.wait()
        gate, up, hidden = (ref[rows].astype(F32) for ref in scratch[:3])
        sigma = jax.nn.sigmoid(gate)
        product = hidden * up * sigma * (1.0 + gate * (1.0 - sigma))
        out_ref[:, rows] = product.T.astype(BF16)


def gate_gradient(gate_pre, up_value, grad_hidden):
    return pl.pallas_call(
        gate_kernel,
        in_specs=[IN_HBM] * 3,
        out_specs=IN_VMEM,
        scratch_shapes=[pltpu.VMEM((1024, 128), BF16)] * 3 + [pltpu.SemaphoreType.DMA((3, 4))],
        out_shape=jax.ShapeDtypeStruct((128, 1024), BF16),
        compiler_params=params(58),
    )(gate_pre, up_value, grad_hidden)


def share_kernel(gates_ref, tokens_hbm, own_ref, right_ref, left_ref, far_ref, tokens, sems):
    m = lax.axis_index("mp")
    copies = []
    for step in range(8):
        column = jnp.bitwise_and(m + (2, 1, 3, 0)[step // 2], 3) * 1024 + step % 2 * 512
        copy = pltpu.make_async_copy(
            tokens_hbm.at[:, pl.ds(pl.multiple_of(column, 512), 512)], tokens.at[step], sems.at[step]
        )
        copy.start()
        copies.append(copy)
    for step, copy in enumerate(copies):
        copy.wait()
        out_ref = (far_ref, right_ref, left_ref, own_ref)[step // 2]
        share = jnp.dot(gates_ref[...], tokens[step], preferred_element_type=F32)
        out_ref[:, step % 2 * 512 : (step % 2 + 1) * 512] = share.astype(out_ref.dtype)


def weight_shares(gates, tokens):
    return pl.pallas_call(
        share_kernel,
        in_specs=[IN_VMEM, IN_HBM],
        out_specs=[IN_VMEM] * 4,
        scratch_shapes=[pltpu.VMEM((8, 1024, 512), BF16), pltpu.SemaphoreType.DMA((8,))],
        out_shape=[jax.ShapeDtypeStruct((128, 1024), F32)]
        + [jax.ShapeDtypeStruct((128, 1024), BF16)] * 3,
        compiler_params=params(54),
        cost_estimate=pl.CostEstimate(flops=1 << 30, bytes_accessed=10 << 20, transcendentals=0),
    )(gates, tokens)


def add_kernel(scale, own_ref, right_ref, left_ref, far_ref, out_ref):
    total = own_ref[...]
    for ref in (right_ref, left_ref, far_ref):
        total += ref[...].astype(F32)
    out_ref[...] = (total * scale).T.astype(BF16)


def add_shares(own, away, scale):
    return pl.pallas_call(
        functools.partial(add_kernel, scale),
        in_specs=[IN_VMEM] * 4,
        out_specs=IN_VMEM,
        out_shape=jax.ShapeDtypeStruct((1024, 128), BF16),
        compiler_params=params(),
    )(own, *away)


def partial_kernel(rows_ref, mine_ref, other_ref, out_ref, rows):
    x, c = lax.axis_index("x"), lax.axis_index("c")
    for k in range(8):
        turn = ((0,) + TURNS)[k % 4]
        source = jnp.bitwise_and(x + turn, 3) * 2 + (c if k < 4 else 1 - c)
        for m in range(4):
            rows[m * 128 : (m + 1) * 128, k * 128 : (k + 1) * 128] = rows_ref[m, source]
    for t in range(2):
        columns = pl.ds(t * 512, 512)
        total = jnp.dot(
            rows[:, :512], mine_ref[:, :, columns].reshape(512, 512), preferred_element_type=F32
        )
        total += jnp.dot(
            rows[:, 512:], other_ref[:, :, columns].reshape(512, 512), preferred_element_type=F32
        )
        out_ref[:, columns] = total.astype(BF16)


def partial_product(rows, mine, other):
    return pl.pallas_call(
        partial_kernel,
        in_specs=[IN_VMEM] * 3,
        out_specs=IN_VMEM,
        scratch_shapes=[pltpu.VMEM((512, 1024), BF16)],
        out_shape=jax.ShapeDtypeStruct((512, 1024), BF16),
        compiler_params=params(),
        cost_estimate=pl.CostEstimate(flops=1 << 30, bytes_accessed=4 << 20, transcendentals=0),
    )(rows, mine, other)


def sum_kernel(pieces_ref, out_ref):
    out_ref[...] = jnp.sum(pieces_ref[...].astype(F32), axis=0).astype(BF16)


def sum_pieces(pieces):
    return pl.pallas_call(
        sum_kernel,
        in_specs=[IN_VMEM],
        out_specs=IN_VMEM,
        out_shape=jax.ShapeDtypeStruct((32, 1024), BF16),
        compiler_params=params(),
    )(pieces)


def always(function, *operands):
    shapes = jax.eval_shape(function, *operands)

    def never(*_):
        return jax.tree.map(lambda shape: jnp.zeros(shape.shape, shape.dtype), shapes)

    return lax.cond(lax.axis_index("x") * 2 + lax.axis_index("c") >= 0, function, never, *operands)


def body(tokens, gate_pre, up_value, grad_hidden, gate_weight):
    norm_factor = float(tokens.shape[0] * lax.axis_size("mp")) ** (-0.5)

    rows = spread_rows(gate_weight).reshape(32, 128, 128)
    rows = lax.all_to_all(rows, ("mp", "x", "c"), 0, 0, tiled=True).reshape(4, 8, 128, 128)

    gates = gate_gradient(gate_pre, up_value, grad_hidden)
    mine = [shift(gates, "x", 4, k) for k in TURNS]
    own, *shares = weight_shares(gates, tokens)
    *mine, own = lax.optimization_barrier((*mine, own))
    away = [shift(share, "mp", 4, -k) for k, share in zip(TURNS, shares)]

    def exchange(rows, *mine):
        mine = jnp.stack(mine)
        partial_sums = partial_product(rows, mine, shift(mine, "c", 2, 1))
        pieces = lax.all_to_all(partial_sums.reshape(16, 32, 1024), ("zl", "y"), 0, 0, tiled=True)
        return sum_pieces(pieces)

    grad_tokens = always(exchange, rows, gates, *mine)
    grad_tokens, own, *away = lax.optimization_barrier((grad_tokens, own, *away))
    return (grad_tokens.T, add_shares(own, away, norm_factor))


def solution(mesh):
    fine = Mesh(mesh.devices.reshape(2, 8, 4, 2, 4), AXES)
    dp = ("zl", "y", "x", "c")
    in_specs = (P("mp", None), P("mp", dp), P("mp", dp), P("mp", dp), P("mp", dp))
    out_specs = (P("mp", dp), P("mp", dp))
    return jax.shard_map(body, mesh=fine, in_specs=in_specs, out_specs=out_specs, check_vma=False)
```

```python
import functools

import jax
import jax.numpy as jnp
from jax import lax
from jax.experimental import pallas as pl
from jax.experimental.pallas import tpu as pltpu
from jax.sharding import Mesh, PartitionSpec as P

TURNS = (1, 3, 2)
AXES = ("zl", "y", "x", "c", "mp")
BF16, F32 = jnp.bfloat16, jnp.float32
IN_HBM = pl.BlockSpec(memory_space=pltpu.HBM)
IN_VMEM = pl.BlockSpec(memory_space=pltpu.VMEM)


def shift(array, axis, size, by):
    return lax.ppermute(array, axis, [((i + by) % size, i) for i in range(size)])


def params(limit=24):
    return pltpu.CompilerParams(vmem_limit_bytes=limit << 20)


def spread_kernel(weight_hbm, out_hbm, weight, spread, sems):
    copy = pltpu.make_async_copy(weight_hbm, weight, sems.at[4])
    copy.start()
    copy.wait()
    for k in range(8):
        for q in range(4):
            spread[k, q * 32 : (q + 1) * 32, :] = weight[(q * 8 + k) * 32 : (q * 8 + k + 1) * 32, :]
    copies = [pltpu.make_async_copy(spread, out_hbm.at[m], sems.at[m]) for m in range(4)]
    for copy in copies:
        copy.start()
    for copy in copies:
        copy.wait()


def spread_rows(weight):
    return pl.pallas_call(
        spread_kernel,
        in_specs=[IN_HBM],
        out_specs=IN_HBM,
        scratch_shapes=[
            pltpu.VMEM((1024, 128), BF16),
            pltpu.VMEM((8, 128, 128), BF16),
            pltpu.SemaphoreType.DMA((5,)),
        ],
        out_shape=jax.ShapeDtypeStruct((4, 8, 128, 128), BF16),
        compiler_params=params(58),
    )(weight)


def gate_kernel(gate_hbm, up_hbm, hidden_hbm, out_ref, *scratch):
    sems = scratch[3]
    copies = []
    for step in range(4):
        rows = pl.ds(step * 256, 256)
        for n, source in enumerate((gate_hbm, up_hbm, hidden_hbm)):
            copy = pltpu.make_async_copy(source.at[rows], scratch[n].at[rows], sems.at[n, step])
            copy.start()
            copies.append(copy)
    for step in range(4):
        rows = pl.ds(step * 256, 256)
        for copy in copies[step * 3 : step * 3 + 3]:
            copy.wait()
        gate, up, hidden = (ref[rows].astype(F32) for ref in scratch[:3])
        sigma = jax.nn.sigmoid(gate)
        product = hidden * up * sigma * (1.0 + gate * (1.0 - sigma))
        out_ref[:, rows] = product.T.astype(BF16)


def gate_gradient(gate_pre, up_value, grad_hidden):
    return pl.pallas_call(
        gate_kernel,
        in_specs=[IN_HBM] * 3,
        out_specs=IN_VMEM,
        scratch_shapes=[pltpu.VMEM((1024, 128), BF16)] * 3 + [pltpu.SemaphoreType.DMA((3, 4))],
        out_shape=jax.ShapeDtypeStruct((128, 1024), BF16),
        compiler_params=params(58),
    )(gate_pre, up_value, grad_hidden)


def share_kernel(gates_ref, tokens_hbm, own_ref, right_ref, left_ref, far_ref, tokens, sems):
    m = lax.axis_index("mp")
    copies = []
    for step in range(8):
        column = jnp.bitwise_and(m + (2, 1, 3, 0)[step // 2], 3) * 1024 + step % 2 * 512
        copy = pltpu.make_async_copy(
            tokens_hbm.at[:, pl.ds(pl.multiple_of(column, 512), 512)], tokens.at[step], sems.at[step]
        )
        copy.start()
        copies.append(copy)
    for step, copy in enumerate(copies):
        copy.wait()
        out_ref = (far_ref, right_ref, left_ref, own_ref)[step // 2]
        share = jnp.dot(gates_ref[...], tokens[step], preferred_element_type=F32)
        out_ref[:, step % 2 * 512 : (step % 2 + 1) * 512] = share.astype(out_ref.dtype)


def weight_shares(gates, tokens):
    return pl.pallas_call(
        share_kernel,
        in_specs=[IN_VMEM, IN_HBM],
        out_specs=[IN_VMEM] * 4,
        scratch_shapes=[pltpu.VMEM((8, 1024, 512), BF16), pltpu.SemaphoreType.DMA((8,))],
        out_shape=[jax.ShapeDtypeStruct((128, 1024), F32)]
        + [jax.ShapeDtypeStruct((128, 1024), BF16)] * 3,
        compiler_params=params(54),
        cost_estimate=pl.CostEstimate(flops=1 << 30, bytes_accessed=10 << 20, transcendentals=0),
    )(gates, tokens)


def add_kernel(scale, own_ref, right_ref, left_ref, far_ref, out_ref):
    total = own_ref[...]
    for ref in (right_ref, left_ref, far_ref):
        total += ref[...].astype(F32)
    out_ref[...] = (total * scale).T.astype(BF16)


def add_shares(own, away, scale):
    return pl.pallas_call(
        functools.partial(add_kernel, scale),
        in_specs=[IN_VMEM] * 4,
        out_specs=IN_VMEM,
        out_shape=jax.ShapeDtypeStruct((1024, 128), BF16),
        compiler_params=params(),
    )(own, *away)


def partial_kernel(rows_ref, mine_ref, other_ref, out_ref, rows):
    x, c = lax.axis_index("x"), lax.axis_index("c")
    for k in range(8):
        source = jnp.bitwise_xor(x, k % 4) * 2 + (c if k < 4 else 1 - c)
        for m in range(4):
            rows[m * 128 : (m + 1) * 128, k * 128 : (k + 1) * 128] = rows_ref[m, source]
    for t in range(2):
        columns = pl.ds(t * 512, 512)
        total = jnp.dot(
            rows[:, :512], mine_ref[:, :, columns].reshape(512, 512), preferred_element_type=F32
        )
        total += jnp.dot(
            rows[:, 512:], other_ref[:, :, columns].reshape(512, 512), preferred_element_type=F32
        )
        out_ref[:, columns] = total.astype(BF16)


def partial_product(rows, mine, other):
    return pl.pallas_call(
        partial_kernel,
        in_specs=[IN_VMEM] * 3,
        out_specs=IN_VMEM,
        scratch_shapes=[pltpu.VMEM((512, 1024), BF16)],
        out_shape=jax.ShapeDtypeStruct((512, 1024), BF16),
        compiler_params=params(),
        cost_estimate=pl.CostEstimate(flops=1 << 30, bytes_accessed=4 << 20, transcendentals=0),
    )(rows, mine, other)


def sum_kernel(pieces_ref, out_ref):
    out_ref[...] = jnp.sum(pieces_ref[...].astype(F32), axis=0).astype(BF16)


def sum_pieces(pieces):
    return pl.pallas_call(
        sum_kernel,
        in_specs=[IN_VMEM],
        out_specs=IN_VMEM,
        out_shape=jax.ShapeDtypeStruct((32, 1024), BF16),
        compiler_params=params(),
    )(pieces)


def always(function, *operands):
    shapes = jax.eval_shape(function, *operands)

    def never(*_):
        return jax.tree.map(lambda shape: jnp.zeros(shape.shape, shape.dtype), shapes)

    return lax.cond(lax.axis_index("x") * 2 + lax.axis_index("c") >= 0, function, never, *operands)


def body(tokens, gate_pre, up_value, grad_hidden, gate_weight):
    norm_factor = float(tokens.shape[0] * lax.axis_size("mp")) ** (-0.5)

    rows = spread_rows(gate_weight).reshape(32, 128, 128)
    rows = lax.all_to_all(rows, ("mp", "x", "c"), 0, 0, tiled=True).reshape(4, 8, 128, 128)

    gates = gate_gradient(gate_pre, up_value, grad_hidden)
    near = lax.ppermute(gates, "x", [(i, i ^ 1) for i in range(4)])
    own, *shares = weight_shares(gates, tokens)
    near, own = lax.optimization_barrier((near, own))
    pair = jnp.stack([gates, near])
    other_pair = lax.ppermute(pair, "x", [(i, i ^ 2) for i in range(4)])
    away = [shift(share, "mp", 4, -k) for k, share in zip(TURNS, shares)]

    def exchange(rows, *pairs):
        mine = jnp.concatenate(pairs)
        partial_sums = partial_product(rows, mine, shift(mine, "c", 2, 1))
        pieces = lax.all_to_all(partial_sums.reshape(16, 32, 1024), ("zl", "y"), 0, 0, tiled=True)
        return sum_pieces(pieces)

    grad_tokens = always(exchange, rows, pair, other_pair)
    grad_tokens, own, *away = lax.optimization_barrier((grad_tokens, own, *away))
    return (grad_tokens.T, add_shares(own, away, norm_factor))


def solution(mesh):
    fine = Mesh(mesh.devices.reshape(2, 8, 4, 2, 4), AXES)
    dp = ("zl", "y", "x", "c")
    in_specs = (P("mp", None), P("mp", dp), P("mp", dp), P("mp", dp), P("mp", dp))
    out_specs = (P("mp", dp), P("mp", dp))
    return jax.shard_map(body, mesh=fine, in_specs=in_specs, out_specs=out_specs, check_vma=False)
```

```python
import functools

import jax
import jax.numpy as jnp
from jax import lax
from jax.experimental import pallas as pl
from jax.experimental.pallas import tpu as pltpu
from jax.sharding import Mesh, PartitionSpec as P

TURNS = (1, 3, 2)
AXES = ("zl", "y", "x", "c", "mp")
BF16, F32 = jnp.bfloat16, jnp.float32
IN_HBM = pl.BlockSpec(memory_space=pltpu.HBM)
IN_VMEM = pl.BlockSpec(memory_space=pltpu.VMEM)


def shift(array, axis, size, by):
    return lax.ppermute(array, axis, [((i + by) % size, i) for i in range(size)])


def params(limit=24):
    return pltpu.CompilerParams(vmem_limit_bytes=limit << 20)


def spread_kernel(weight_hbm, out_hbm, weight, spread, sems):
    copy = pltpu.make_async_copy(weight_hbm, weight, sems.at[4])
    copy.start()
    copy.wait()
    for k in range(8):
        for q in range(4):
            spread[k, q * 32 : (q + 1) * 32, :] = weight[(q * 8 + k) * 32 : (q * 8 + k + 1) * 32, :]
    copies = [pltpu.make_async_copy(spread, out_hbm.at[:, m], sems.at[m]) for m in range(4)]
    for copy in copies:
        copy.start()
    for copy in copies:
        copy.wait()


def spread_rows(weight):
    return pl.pallas_call(
        spread_kernel,
        in_specs=[IN_HBM],
        out_specs=IN_HBM,
        scratch_shapes=[
            pltpu.VMEM((1024, 128), BF16),
            pltpu.VMEM((8, 128, 128), BF16),
            pltpu.SemaphoreType.DMA((5,)),
        ],
        out_shape=jax.ShapeDtypeStruct((8, 4, 128, 128), BF16),
        compiler_params=params(58),
    )(weight)


def gate_kernel(gate_hbm, up_hbm, hidden_hbm, out_ref, *scratch):
    sems = scratch[3]
    copies = []
    for step in range(4):
        rows = pl.ds(step * 256, 256)
        for n, source in enumerate((gate_hbm, up_hbm, hidden_hbm)):
            copy = pltpu.make_async_copy(source.at[rows], scratch[n].at[rows], sems.at[n, step])
            copy.start()
            copies.append(copy)
    for step in range(4):
        rows = pl.ds(step * 256, 256)
        for copy in copies[step * 3 : step * 3 + 3]:
            copy.wait()
        gate, up, hidden = (ref[rows].astype(F32) for ref in scratch[:3])
        sigma = jax.nn.sigmoid(gate)
        product = hidden * up * sigma * (1.0 + gate * (1.0 - sigma))
        out_ref[:, rows] = product.T.astype(BF16)


def gate_gradient(gate_pre, up_value, grad_hidden):
    return pl.pallas_call(
        gate_kernel,
        in_specs=[IN_HBM] * 3,
        out_specs=IN_VMEM,
        scratch_shapes=[pltpu.VMEM((1024, 128), BF16)] * 3 + [pltpu.SemaphoreType.DMA((3, 4))],
        out_shape=jax.ShapeDtypeStruct((128, 1024), BF16),
        compiler_params=params(58),
    )(gate_pre, up_value, grad_hidden)


def share_kernel(gates_ref, tokens_hbm, own_ref, right_ref, left_ref, far_ref, tokens, sems):
    m = lax.axis_index("mp")
    copies = []
    for step in range(8):
        column = jnp.bitwise_and(m + (2, 1, 3, 0)[step // 2], 3) * 1024 + step % 2 * 512
        copy = pltpu.make_async_copy(
            tokens_hbm.at[:, pl.ds(pl.multiple_of(column, 512), 512)], tokens.at[step], sems.at[step]
        )
        copy.start()
        copies.append(copy)
    for step, copy in enumerate(copies):
        copy.wait()
        out_ref = (far_ref, right_ref, left_ref, own_ref)[step // 2]
        share = jnp.dot(gates_ref[...], tokens[step], preferred_element_type=F32)
        out_ref[:, step % 2 * 512 : (step % 2 + 1) * 512] = share.astype(out_ref.dtype)


def weight_shares(gates, tokens):
    return pl.pallas_call(
        share_kernel,
        in_specs=[IN_VMEM, IN_HBM],
        out_specs=[IN_VMEM] * 4,
        scratch_shapes=[pltpu.VMEM((8, 1024, 512), BF16), pltpu.SemaphoreType.DMA((8,))],
        out_shape=[jax.ShapeDtypeStruct((128, 1024), F32)]
        + [jax.ShapeDtypeStruct((128, 1024), BF16)] * 3,
        compiler_params=params(54),
        cost_estimate=pl.CostEstimate(flops=1 << 30, bytes_accessed=10 << 20, transcendentals=0),
    )(gates, tokens)


def add_kernel(scale, own_ref, right_ref, left_ref, far_ref, out_ref):
    total = own_ref[...]
    for ref in (right_ref, left_ref, far_ref):
        total += ref[...].astype(F32)
    out_ref[...] = (total * scale).T.astype(BF16)


def add_shares(own, away, scale):
    return pl.pallas_call(
        functools.partial(add_kernel, scale),
        in_specs=[IN_VMEM] * 4,
        out_specs=IN_VMEM,
        out_shape=jax.ShapeDtypeStruct((1024, 128), BF16),
        compiler_params=params(),
    )(own, *away)


def partial_kernel(rows_ref, mine_ref, other_ref, out_ref, rows):
    x, c = lax.axis_index("x"), lax.axis_index("c")
    for k in range(8):
        turn = ((0,) + TURNS)[k % 4]
        source = jnp.bitwise_and(x + turn, 3) * 2 + (c if k < 4 else 1 - c)
        for q in range(16):
            at = ((q // 4 % 2 * 4 + q % 4) * 2 + q // 8) * 32
            piece = rows_ref[source, q // 4, q % 4 * 32 : (q % 4 + 1) * 32, :]
            rows[at : at + 32, k * 128 : (k + 1) * 128] = piece
    for t in range(2):
        columns = pl.ds(t * 512, 512)
        total = jnp.dot(
            rows[:, :512], mine_ref[:, :, columns].reshape(512, 512), preferred_element_type=F32
        )
        total += jnp.dot(
            rows[:, 512:], other_ref[:, :, columns].reshape(512, 512), preferred_element_type=F32
        )
        out_ref[:, columns] = total.astype(BF16)


def partial_product(rows, mine, other):
    return pl.pallas_call(
        partial_kernel,
        in_specs=[IN_VMEM] * 3,
        out_specs=IN_VMEM,
        scratch_shapes=[pltpu.VMEM((512, 1024), BF16)],
        out_shape=jax.ShapeDtypeStruct((512, 1024), BF16),
        compiler_params=params(),
        cost_estimate=pl.CostEstimate(flops=1 << 30, bytes_accessed=4 << 20, transcendentals=0),
    )(rows, mine, other)


def sum_kernel(pieces_ref, out_ref):
    out_ref[...] = jnp.sum(pieces_ref[...].astype(F32), axis=0).astype(BF16)


def sum_pieces(pieces):
    return pl.pallas_call(
        sum_kernel,
        in_specs=[IN_VMEM],
        out_specs=IN_VMEM,
        out_shape=jax.ShapeDtypeStruct((32, 1024), BF16),
        compiler_params=params(),
    )(pieces)


def always(function, *operands):
    shapes = jax.eval_shape(function, *operands)

    def never(*_):
        return jax.tree.map(lambda shape: jnp.zeros(shape.shape, shape.dtype), shapes)

    return lax.cond(lax.axis_index("x") * 2 + lax.axis_index("c") >= 0, function, never, *operands)


def body(tokens, gate_pre, up_value, grad_hidden, gate_weight):
    norm_factor = float(tokens.shape[0] * lax.axis_size("mp")) ** (-0.5)

    rows = spread_rows(gate_weight).reshape(32, 128, 128)
    rows = lax.all_to_all(rows, ("x", "c", "mp"), 0, 0, tiled=True).reshape(8, 4, 128, 128)

    gates = gate_gradient(gate_pre, up_value, grad_hidden)
    mine = [shift(gates, "x", 4, k) for k in TURNS]
    own, *shares = weight_shares(gates, tokens)
    *mine, own = lax.optimization_barrier((*mine, own))
    away = [shift(share, "mp", 4, -k) for k, share in zip(TURNS, shares)]

    def exchange(rows, *mine):
        mine = jnp.stack(mine)
        partial_sums = partial_product(rows, mine, shift(mine, "c", 2, 1))
        pieces = lax.all_to_all(partial_sums.reshape(16, 32, 1024), ("y", "zl"), 0, 0, tiled=True)
        return sum_pieces(pieces)

    grad_tokens = always(exchange, rows, gates, *mine)
    grad_tokens, own, *away = lax.optimization_barrier((grad_tokens, own, *away))
    return (grad_tokens.T, add_shares(own, away, norm_factor))


def solution(mesh):
    fine = Mesh(mesh.devices.reshape(2, 8, 4, 2, 4), AXES)
    dp = ("zl", "y", "x", "c")
    in_specs = (P("mp", None), P("mp", dp), P("mp", dp), P("mp", dp), P("mp", dp))
    out_specs = (P("mp", dp), P("mp", dp))
    return jax.shard_map(body, mesh=fine, in_specs=in_specs, out_specs=out_specs, check_vma=False)
```

```python
import functools

import jax
import jax.numpy as jnp
from jax import lax
from jax.experimental import pallas as pl
from jax.experimental.pallas import tpu as pltpu
from jax.sharding import Mesh, PartitionSpec as P

TURNS = (1, 3, 2)
AXES = ("zl", "y", "x", "c", "mp")
BF16, F32 = jnp.bfloat16, jnp.float32
IN_HBM = pl.BlockSpec(memory_space=pltpu.HBM)
IN_VMEM = pl.BlockSpec(memory_space=pltpu.VMEM)


def shift(array, axis, size, by):
    return lax.ppermute(array, axis, [((i + by) % size, i) for i in range(size)])


def params(limit=24):
    return pltpu.CompilerParams(vmem_limit_bytes=limit << 20)


def spread_kernel(weight_hbm, out_hbm, weight, spread, sems):
    copy = pltpu.make_async_copy(weight_hbm, weight, sems.at[4])
    copy.start()
    copy.wait()
    for k in range(8):
        for q in range(4):
            spread[k, q * 32 : (q + 1) * 32, :] = weight[(q * 8 + k) * 32 : (q * 8 + k + 1) * 32, :]
    copies = [pltpu.make_async_copy(spread, out_hbm.at[m], sems.at[m]) for m in range(4)]
    for copy in copies:
        copy.start()
    for copy in copies:
        copy.wait()


def spread_rows(weight):
    return pl.pallas_call(
        spread_kernel,
        in_specs=[IN_HBM],
        out_specs=IN_HBM,
        scratch_shapes=[
            pltpu.VMEM((1024, 128), BF16),
            pltpu.VMEM((8, 128, 128), BF16),
            pltpu.SemaphoreType.DMA((5,)),
        ],
        out_shape=jax.ShapeDtypeStruct((4, 8, 128, 128), BF16),
        compiler_params=params(58),
    )(weight)


def gate_kernel(gate_hbm, up_hbm, hidden_hbm, tokens_hbm, gates_ref, own_ref, right_ref, left_ref, far_ref, *scratch):
    inputs, tokens, sems = scratch[:3], scratch[3], scratch[4]
    m = lax.axis_index("mp")
    copies, arrivals = [], []
    for step in range(4):
        rows = pl.ds(step * 256, 256)
        for n, source in enumerate((gate_hbm, up_hbm, hidden_hbm)):
            copies.append(
                pltpu.make_async_copy(source.at[rows], inputs[n].at[rows], sems.at[step * 3 + n])
            )
    for step in range(8):
        column = jnp.bitwise_and(m + (2, 1, 3, 0)[step // 2], 3) * 1024 + step % 2 * 512
        arrivals.append(
            pltpu.make_async_copy(
                tokens_hbm.at[:, pl.ds(pl.multiple_of(column, 512), 512)],
                tokens.at[step],
                sems.at[12 + step],
            )
        )
    for copy in copies + arrivals:
        copy.start()
    for step in range(4):
        rows = pl.ds(step * 256, 256)
        for copy in copies[step * 3 : step * 3 + 3]:
            copy.wait()
        gate, up, hidden = (ref[rows].astype(F32) for ref in inputs)
        sigma = jax.nn.sigmoid(gate)
        product = hidden * up * sigma * (1.0 + gate * (1.0 - sigma))
        gates_ref[:, rows] = product.T.astype(BF16)
    for step, copy in enumerate(arrivals):
        copy.wait()
        out_ref = (far_ref, right_ref, left_ref, own_ref)[step // 2]
        share = jnp.dot(gates_ref[...], tokens[step], preferred_element_type=F32)
        out_ref[:, step % 2 * 512 : (step % 2 + 1) * 512] = share.astype(out_ref.dtype)


def gates_and_shares(gate_pre, up_value, grad_hidden, tokens):
    part = jax.ShapeDtypeStruct((128, 1024), BF16)
    return pl.pallas_call(
        gate_kernel,
        in_specs=[IN_HBM] * 4,
        out_specs=[IN_VMEM] * 5,
        scratch_shapes=[pltpu.VMEM((1024, 128), BF16)] * 3
        + [pltpu.VMEM((8, 1024, 512), BF16), pltpu.SemaphoreType.DMA((20,))],
        out_shape=[part, jax.ShapeDtypeStruct((128, 1024), F32), part, part, part],
        compiler_params=params(54),
        cost_estimate=pl.CostEstimate(flops=1 << 30, bytes_accessed=10 << 20, transcendentals=0),
    )(gate_pre, up_value, grad_hidden, tokens)


def add_kernel(scale, own_ref, right_ref, left_ref, far_ref, out_ref):
    total = own_ref[...]
    for ref in (right_ref, left_ref, far_ref):
        total += ref[...].astype(F32)
    out_ref[...] = (total * scale).T.astype(BF16)


def add_shares(own, away, scale):
    return pl.pallas_call(
        functools.partial(add_kernel, scale),
        in_specs=[IN_VMEM] * 4,
        out_specs=IN_VMEM,
        out_shape=jax.ShapeDtypeStruct((1024, 128), BF16),
        compiler_params=params(),
    )(own, *away)


def partial_kernel(rows_ref, mine_ref, other_ref, out_ref, rows):
    x, c = lax.axis_index("x"), lax.axis_index("c")
    for k in range(8):
        turn = ((0,) + TURNS)[k % 4]
        source = jnp.bitwise_and(x + turn, 3) * 2 + (c if k < 4 else 1 - c)
        for m in range(4):
            rows[m * 128 : (m + 1) * 128, k * 128 : (k + 1) * 128] = rows_ref[m, source]
    for t in range(2):
        columns = pl.ds(t * 512, 512)
        total = jnp.dot(
            rows[:, :512], mine_ref[:, :, columns].reshape(512, 512), preferred_element_type=F32
        )
        total += jnp.dot(
            rows[:, 512:], other_ref[:, :, columns].reshape(512, 512), preferred_element_type=F32
        )
        out_ref[:, columns] = total.astype(BF16)


def partial_product(rows, mine, other):
    return pl.pallas_call(
        partial_kernel,
        in_specs=[IN_VMEM] * 3,
        out_specs=IN_VMEM,
        scratch_shapes=[pltpu.VMEM((512, 1024), BF16)],
        out_shape=jax.ShapeDtypeStruct((512, 1024), BF16),
        compiler_params=params(),
        cost_estimate=pl.CostEstimate(flops=1 << 30, bytes_accessed=4 << 20, transcendentals=0),
    )(rows, mine, other)


def sum_kernel(pieces_ref, out_ref):
    out_ref[...] = jnp.sum(pieces_ref[...].astype(F32), axis=0).astype(BF16)


def sum_pieces(pieces):
    return pl.pallas_call(
        sum_kernel,
        in_specs=[IN_VMEM],
        out_specs=IN_VMEM,
        out_shape=jax.ShapeDtypeStruct((32, 1024), BF16),
        compiler_params=params(),
    )(pieces)


def always(function, *operands):
    shapes = jax.eval_shape(function, *operands)

    def never(*_):
        return jax.tree.map(lambda shape: jnp.zeros(shape.shape, shape.dtype), shapes)

    return lax.cond(lax.axis_index("x") * 2 + lax.axis_index("c") >= 0, function, never, *operands)


def body(tokens, gate_pre, up_value, grad_hidden, gate_weight):
    norm_factor = float(tokens.shape[0] * lax.axis_size("mp")) ** (-0.5)

    rows = spread_rows(gate_weight).reshape(32, 128, 128)
    rows = lax.all_to_all(rows, ("mp", "x", "c"), 0, 0, tiled=True).reshape(4, 8, 128, 128)

    gates, own, right, left, far = gates_and_shares(gate_pre, up_value, grad_hidden, tokens)
    mine = [shift(gates, "x", 4, k) for k in TURNS]
    right, left = shift(right, "mp", 4, -1), shift(left, "mp", 4, 1)

    def exchange(rows, mine, other):
        partial_sums = partial_product(rows, mine, other)
        pieces = lax.all_to_all(partial_sums.reshape(16, 32, 1024), ("zl", "y"), 0, 0, tiled=True)
        return sum_pieces(pieces)

    def cross(rows, far, mine):
        other = shift(mine, "c", 2, 1)
        far = shift(far, "mp", 4, 2)
        total = always(exchange, rows, mine, other)
        return lax.optimization_barrier((total, far))

    grad_tokens, far = always(cross, rows, far, jnp.stack([gates, *mine]))
    grad_tokens, own, right, left, far = lax.optimization_barrier((grad_tokens, own, right, left, far))
    return (grad_tokens.T, add_shares(own, (right, left, far), norm_factor))


def solution(mesh):
    fine = Mesh(mesh.devices.reshape(2, 8, 4, 2, 4), AXES)
    dp = ("zl", "y", "x", "c")
    in_specs = (P("mp", None), P("mp", dp), P("mp", dp), P("mp", dp), P("mp", dp))
    out_specs = (P("mp", dp), P("mp", dp))
    return jax.shard_map(body, mesh=fine, in_specs=in_specs, out_specs=out_specs, check_vma=False)
```

```python
import functools

import jax
import jax.numpy as jnp
from jax import lax
from jax.experimental import pallas as pl
from jax.experimental.pallas import tpu as pltpu
from jax.sharding import Mesh, PartitionSpec as P

TURNS = (1, 3, 2)
AXES = ("zl", "y", "x", "c", "mp")
BF16, F32 = jnp.bfloat16, jnp.float32
IN_HBM = pl.BlockSpec(memory_space=pltpu.HBM)
IN_VMEM = pl.BlockSpec(memory_space=pltpu.VMEM)


def shift(array, axis, size, by):
    return lax.ppermute(array, axis, [((i + by) % size, i) for i in range(size)])


def params(limit=24):
    return pltpu.CompilerParams(vmem_limit_bytes=limit << 20)


def spread_kernel(weight_hbm, out_hbm, weight, spread, sems):
    copy = pltpu.make_async_copy(weight_hbm, weight, sems.at[4])
    copy.start()
    copy.wait()
    for k in range(8):
        for q in range(4):
            spread[k, q * 32 : (q + 1) * 32, :] = weight[(q * 8 + k) * 32 : (q * 8 + k + 1) * 32, :]
    copies = [pltpu.make_async_copy(spread, out_hbm.at[m], sems.at[m]) for m in range(4)]
    for copy in copies:
        copy.start()
    for copy in copies:
        copy.wait()


def spread_rows(weight):
    return pl.pallas_call(
        spread_kernel,
        in_specs=[IN_HBM],
        out_specs=IN_HBM,
        scratch_shapes=[
            pltpu.VMEM((1024, 128), BF16),
            pltpu.VMEM((8, 128, 128), BF16),
            pltpu.SemaphoreType.DMA((5,)),
        ],
        out_shape=jax.ShapeDtypeStruct((4, 8, 128, 128), BF16),
        compiler_params=params(58),
    )(weight)


def gate_kernel(gate_hbm, up_hbm, hidden_hbm, out_ref, *scratch):
    sems = scratch[3]
    copies = []
    for step in range(4):
        rows = pl.ds(step * 256, 256)
        for n, source in enumerate((gate_hbm, up_hbm, hidden_hbm)):
            copy = pltpu.make_async_copy(source.at[rows], scratch[n].at[rows], sems.at[n, step])
            copy.start()
            copies.append(copy)
    for step in range(4):
        rows = pl.ds(step * 256, 256)
        for copy in copies[step * 3 : step * 3 + 3]:
            copy.wait()
        gate, up, hidden = (ref[rows].astype(F32) for ref in scratch[:3])
        sigma = jax.nn.sigmoid(gate)
        product = hidden * up * sigma * (1.0 + gate * (1.0 - sigma))
        out_ref[:, rows] = product.T.astype(BF16)


def gate_gradient(gate_pre, up_value, grad_hidden):
    return pl.pallas_call(
        gate_kernel,
        in_specs=[IN_HBM] * 3,
        out_specs=IN_VMEM,
        scratch_shapes=[pltpu.VMEM((1024, 128), BF16)] * 3 + [pltpu.SemaphoreType.DMA((3, 4))],
        out_shape=jax.ShapeDtypeStruct((128, 1024), BF16),
        compiler_params=params(58),
    )(gate_pre, up_value, grad_hidden)


def share_kernel(gates_ref, tokens_hbm, own_ref, right_ref, left_ref, far_ref, tokens, sems):
    m = lax.axis_index("mp")
    copies = []
    for step in range(8):
        column = jnp.bitwise_and(m + (2, 1, 3, 0)[step // 2], 3) * 1024 + step % 2 * 512
        copy = pltpu.make_async_copy(
            tokens_hbm.at[:, pl.ds(pl.multiple_of(column, 512), 512)], tokens.at[step], sems.at[step]
        )
        copy.start()
        copies.append(copy)
    for step, copy in enumerate(copies):
        copy.wait()
        out_ref = (far_ref, right_ref, left_ref, own_ref)[step // 2]
        share = jnp.dot(gates_ref[...], tokens[step], preferred_element_type=F32)
        out_ref[:, step % 2 * 512 : (step % 2 + 1) * 512] = share.astype(out_ref.dtype)


def weight_shares(gates, tokens):
    return pl.pallas_call(
        share_kernel,
        in_specs=[IN_VMEM, IN_HBM],
        out_specs=[IN_VMEM] * 4,
        scratch_shapes=[pltpu.VMEM((8, 1024, 512), BF16), pltpu.SemaphoreType.DMA((8,))],
        out_shape=[jax.ShapeDtypeStruct((128, 1024), F32)]
        + [jax.ShapeDtypeStruct((128, 1024), BF16)] * 3,
        compiler_params=params(54),
        cost_estimate=pl.CostEstimate(flops=1 << 30, bytes_accessed=10 << 20, transcendentals=0),
    )(gates, tokens)


def add_kernel(scale, own_ref, first_ref, second_ref, third_ref, out_ref):
    total = own_ref[...]
    for ref in (first_ref, second_ref, third_ref):
        total += ref[...].astype(F32)
    out_ref[...] = (total * scale).T.astype(BF16)


def add_shares(own, away, scale):
    return pl.pallas_call(
        functools.partial(add_kernel, scale),
        in_specs=[IN_VMEM] * 4,
        out_specs=IN_VMEM,
        out_shape=jax.ShapeDtypeStruct((1024, 128), BF16),
        compiler_params=params(),
    )(own, *away)


def partial_kernel(rows_ref, mine_ref, other_ref, out_ref, rows):
    x, c = lax.axis_index("x"), lax.axis_index("c")
    for k in range(8):
        turn = ((0,) + TURNS)[k % 4]
        source = jnp.bitwise_and(x + turn, 3) * 2 + (c if k < 4 else 1 - c)
        for m in range(4):
            rows[m * 128 : (m + 1) * 128, k * 128 : (k + 1) * 128] = rows_ref[m, source]
    for t in range(2):
        columns = pl.ds(t * 512, 512)
        total = jnp.dot(
            rows[:, :512], mine_ref[:, :, columns].reshape(512, 512), preferred_element_type=F32
        )
        total += jnp.dot(
            rows[:, 512:], other_ref[:, :, columns].reshape(512, 512), preferred_element_type=F32
        )
        out_ref[:, columns] = total.astype(BF16)


def partial_product(rows, mine, other):
    return pl.pallas_call(
        partial_kernel,
        in_specs=[IN_VMEM] * 3,
        out_specs=IN_VMEM,
        scratch_shapes=[pltpu.VMEM((512, 1024), BF16)],
        out_shape=jax.ShapeDtypeStruct((512, 1024), BF16),
        compiler_params=params(),
        cost_estimate=pl.CostEstimate(flops=1 << 30, bytes_accessed=4 << 20, transcendentals=0),
    )(rows, mine, other)


def sum_kernel(pieces_ref, out_ref):
    out_ref[...] = jnp.sum(pieces_ref[...].astype(F32), axis=0).astype(BF16)


def sum_pieces(pieces):
    return pl.pallas_call(
        sum_kernel,
        in_specs=[IN_VMEM],
        out_specs=IN_VMEM,
        out_shape=jax.ShapeDtypeStruct((32, 1024), BF16),
        compiler_params=params(),
    )(pieces)


def always(function, *operands):
    shapes = jax.eval_shape(function, *operands)

    def never(*_):
        return jax.tree.map(lambda shape: jnp.zeros(shape.shape, shape.dtype), shapes)

    return lax.cond(lax.axis_index("x") * 2 + lax.axis_index("c") >= 0, function, never, *operands)


def body(tokens, gate_pre, up_value, grad_hidden, gate_weight):
    norm_factor = float(tokens.shape[0] * lax.axis_size("mp")) ** (-0.5)

    rows = spread_rows(gate_weight).reshape(32, 128, 128)
    rows = lax.all_to_all(rows, ("mp", "x", "c"), 0, 0, tiled=True).reshape(4, 8, 128, 128)

    gates = gate_gradient(gate_pre, up_value, grad_hidden)
    mine = [shift(gates, "x", 4, k) for k in TURNS]
    own, *shares = weight_shares(gates, tokens)
    *mine, own = lax.optimization_barrier((*mine, own))
    right, left, far = shares
    far = shift(far, "mp", 4, 2)
    away = far, shift(right, "mp", 4, -1), shift(left, "mp", 4, 1)

    def exchange(rows, *mine):
        mine = jnp.stack(mine)
        partial_sums = partial_product(rows, mine, shift(mine, "c", 2, 1))
        pieces = lax.all_to_all(partial_sums.reshape(16, 32, 1024), ("zl", "y"), 0, 0, tiled=True)
        return sum_pieces(pieces)

    grad_tokens = always(exchange, rows, gates, *mine)
    grad_tokens, own, *away = lax.optimization_barrier((grad_tokens, own, *away))
    return (grad_tokens.T, add_shares(own, away, norm_factor))


def solution(mesh):
    fine = Mesh(mesh.devices.reshape(2, 8, 4, 2, 4), AXES)
    dp = ("zl", "y", "x", "c")
    in_specs = (P("mp", None), P("mp", dp), P("mp", dp), P("mp", dp), P("mp", dp))
    out_specs = (P("mp", dp), P("mp", dp))
    return jax.shard_map(body, mesh=fine, in_specs=in_specs, out_specs=out_specs, check_vma=False)
```

```python
import functools

import jax
import jax.numpy as jnp
from jax import lax
from jax.experimental import pallas as pl
from jax.experimental.pallas import tpu as pltpu
from jax.sharding import Mesh, PartitionSpec as P

TURNS = (1, 3, 2)
AXES = ("zl", "y", "x", "c", "mp")
BF16, F32 = jnp.bfloat16, jnp.float32
IN_HBM = pl.BlockSpec(memory_space=pltpu.HBM)
IN_VMEM = pl.BlockSpec(memory_space=pltpu.VMEM)


def shift(array, axis, size, by):
    return lax.ppermute(array, axis, [((i + by) % size, i) for i in range(size)])


def params(limit=24):
    return pltpu.CompilerParams(vmem_limit_bytes=limit << 20)


def spread_kernel(weight_hbm, out_hbm, weight, spread, sems):
    copy = pltpu.make_async_copy(weight_hbm, weight, sems.at[4])
    copy.start()
    copy.wait()
    for k in range(8):
        for q in range(4):
            spread[k, q * 32 : (q + 1) * 32, :] = weight[(q * 8 + k) * 32 : (q * 8 + k + 1) * 32, :]
    copies = [pltpu.make_async_copy(spread, out_hbm.at[m], sems.at[m]) for m in range(4)]
    for copy in copies:
        copy.start()
    for copy in copies:
        copy.wait()


def spread_rows(weight):
    return pl.pallas_call(
        spread_kernel,
        in_specs=[IN_HBM],
        out_specs=IN_HBM,
        scratch_shapes=[
            pltpu.VMEM((1024, 128), BF16),
            pltpu.VMEM((8, 128, 128), BF16),
            pltpu.SemaphoreType.DMA((5,)),
        ],
        out_shape=jax.ShapeDtypeStruct((4, 8, 128, 128), BF16),
        compiler_params=params(58),
    )(weight)


def gate_kernel(gate_hbm, up_hbm, hidden_hbm, out_ref, *scratch):
    sems = scratch[3]
    copies = []
    for step in range(4):
        rows = pl.ds(step * 256, 256)
        for n, source in enumerate((gate_hbm, up_hbm, hidden_hbm)):
            copy = pltpu.make_async_copy(source.at[rows], scratch[n].at[rows], sems.at[n, step])
            copy.start()
            copies.append(copy)
    for step in range(4):
        rows = pl.ds(step * 256, 256)
        for copy in copies[step * 3 : step * 3 + 3]:
            copy.wait()
        gate, up, hidden = (ref[rows].astype(F32) for ref in scratch[:3])
        sigma = jax.nn.sigmoid(gate)
        product = hidden * up * sigma * (1.0 + gate * (1.0 - sigma))
        out_ref[:, rows] = product.T.astype(BF16)


def gate_gradient(gate_pre, up_value, grad_hidden):
    return pl.pallas_call(
        gate_kernel,
        in_specs=[IN_HBM] * 3,
        out_specs=IN_VMEM,
        scratch_shapes=[pltpu.VMEM((1024, 128), BF16)] * 3 + [pltpu.SemaphoreType.DMA((3, 4))],
        out_shape=jax.ShapeDtypeStruct((128, 1024), BF16),
        compiler_params=params(58),
    )(gate_pre, up_value, grad_hidden)


def share_kernel(gates_ref, tokens_hbm, own_ref, right_ref, left_ref, far_ref, tokens, sems):
    m = lax.axis_index("mp")
    copies = []
    for step in range(8):
        column = jnp.bitwise_and(m + (2, 1, 3, 0)[step // 2], 3) * 1024 + step % 2 * 512
        copy = pltpu.make_async_copy(
            tokens_hbm.at[:, pl.ds(pl.multiple_of(column, 512), 512)], tokens.at[step], sems.at[step]
        )
        copy.start()
        copies.append(copy)
    for step, copy in enumerate(copies):
        copy.wait()
        out_ref = (far_ref, right_ref, left_ref, own_ref)[step // 2]
        share = jnp.dot(gates_ref[...], tokens[step], preferred_element_type=F32)
        out_ref[:, step % 2 * 512 : (step % 2 + 1) * 512] = share.astype(out_ref.dtype)


def weight_shares(gates, tokens):
    return pl.pallas_call(
        share_kernel,
        in_specs=[IN_VMEM, IN_HBM],
        out_specs=[IN_VMEM] * 4,
        scratch_shapes=[pltpu.VMEM((8, 1024, 512), BF16), pltpu.SemaphoreType.DMA((8,))],
        out_shape=[jax.ShapeDtypeStruct((128, 1024), F32)]
        + [jax.ShapeDtypeStruct((128, 1024), BF16)] * 3,
        compiler_params=params(54),
        cost_estimate=pl.CostEstimate(flops=1 << 30, bytes_accessed=10 << 20, transcendentals=0),
    )(gates, tokens)


def add_kernel(scale, own_ref, right_ref, left_ref, far_ref, out_ref):
    total = own_ref[...]
    for ref in (right_ref, left_ref, far_ref):
        total += ref[...].astype(F32)
    out_ref[...] = (total * scale).T.astype(BF16)


def add_shares(own, away, scale):
    return pl.pallas_call(
        functools.partial(add_kernel, scale),
        in_specs=[IN_VMEM] * 4,
        out_specs=IN_VMEM,
        out_shape=jax.ShapeDtypeStruct((1024, 128), BF16),
        compiler_params=params(),
    )(own, *away)


def partial_kernel(rows_ref, mine_ref, other_ref, out_ref, rows):
    x, c = lax.axis_index("x"), lax.axis_index("c")
    for k in range(8):
        turn = ((0,) + TURNS)[k % 4]
        source = jnp.bitwise_and(x + turn, 3) * 2 + (c if k < 4 else 1 - c)
        for m in range(4):
            rows[m * 128 : (m + 1) * 128, k * 128 : (k + 1) * 128] = rows_ref[m, source]
    for t in range(2):
        columns = pl.ds(t * 512, 512)
        total = jnp.dot(
            rows[:, :512], mine_ref[:, :, columns].reshape(512, 512), preferred_element_type=F32
        )
        total += jnp.dot(
            rows[:, 512:], other_ref[:, :, columns].reshape(512, 512), preferred_element_type=F32
        )
        out_ref[:, columns] = total.astype(BF16)


def partial_product(rows, mine, other):
    return pl.pallas_call(
        partial_kernel,
        in_specs=[IN_VMEM] * 3,
        out_specs=IN_VMEM,
        scratch_shapes=[pltpu.VMEM((512, 1024), BF16)],
        out_shape=jax.ShapeDtypeStruct((512, 1024), BF16),
        compiler_params=params(),
        cost_estimate=pl.CostEstimate(flops=1 << 30, bytes_accessed=4 << 20, transcendentals=0),
    )(rows, mine, other)


def sum_kernel(pieces_ref, out_ref):
    out_ref[...] = jnp.sum(pieces_ref[...].astype(F32), axis=0).astype(BF16)


def sum_pieces(pieces):
    return pl.pallas_call(
        sum_kernel,
        in_specs=[IN_VMEM],
        out_specs=IN_VMEM,
        out_shape=jax.ShapeDtypeStruct((32, 1024), BF16),
        compiler_params=params(),
    )(pieces)


def always(function, *operands):
    shapes = jax.eval_shape(function, *operands)

    def never(*_):
        return jax.tree.map(lambda shape: jnp.zeros(shape.shape, shape.dtype), shapes)

    return lax.cond(lax.axis_index("x") * 2 + lax.axis_index("c") >= 0, function, never, *operands)


def body(tokens, gate_pre, up_value, grad_hidden, gate_weight):
    norm_factor = float(tokens.shape[0] * lax.axis_size("mp")) ** (-0.5)

    rows = spread_rows(gate_weight).reshape(32, 128, 128)
    rows = lax.all_to_all(rows, ("mp", "x", "c"), 0, 0, tiled=True).reshape(4, 8, 128, 128)

    gates = gate_gradient(gate_pre, up_value, grad_hidden)
    mine = [shift(gates, "x", 4, k) for k in TURNS]
    own, *shares = weight_shares(gates, tokens)
    *mine, own = lax.optimization_barrier((*mine, own))
    right, left, far = shares
    right, far = shift(right, "mp", 4, -1), shift(far, "mp", 4, 2)

    def exchange(rows, left, *mine):
        mine = jnp.stack(mine)
        partial_sums = partial_product(rows, mine, shift(mine, "c", 2, 1))
        pieces = lax.all_to_all(partial_sums.reshape(16, 32, 1024), ("zl", "y"), 0, 0, tiled=True)
        return sum_pieces(pieces), shift(left, "mp", 4, 1)

    grad_tokens, left = always(exchange, rows, left, gates, *mine)
    grad_tokens, own, right, left, far = lax.optimization_barrier((grad_tokens, own, right, left, far))
    return (grad_tokens.T, add_shares(own, (right, left, far), norm_factor))


def solution(mesh):
    fine = Mesh(mesh.devices.reshape(2, 8, 4, 2, 4), AXES)
    dp = ("zl", "y", "x", "c")
    in_specs = (P("mp", None), P("mp", dp), P("mp", dp), P("mp", dp), P("mp", dp))
    out_specs = (P("mp", dp), P("mp", dp))
    return jax.shard_map(body, mesh=fine, in_specs=in_specs, out_specs=out_specs, check_vma=False)
```

```python
import functools

import jax
import jax.numpy as jnp
from jax import lax
from jax.experimental import pallas as pl
from jax.experimental.pallas import tpu as pltpu
from jax.sharding import Mesh, PartitionSpec as P

TURNS = (1, 3, 2)
AXES = ("zl", "y", "x", "c", "mp")
BF16, F32 = jnp.bfloat16, jnp.float32
IN_HBM = pl.BlockSpec(memory_space=pltpu.HBM)
IN_VMEM = pl.BlockSpec(memory_space=pltpu.VMEM)


def shift(array, axis, size, by):
    return lax.ppermute(array, axis, [((i + by) % size, i) for i in range(size)])


def params(limit=24):
    return pltpu.CompilerParams(vmem_limit_bytes=limit << 20)


def spread_kernel(weight_hbm, out_hbm, weight, spread, sems):
    copy = pltpu.make_async_copy(weight_hbm, weight, sems.at[4])
    copy.start()
    copy.wait()
    for k in range(8):
        for q in range(4):
            spread[k, q * 32 : (q + 1) * 32, :] = weight[(q * 8 + k) * 32 : (q * 8 + k + 1) * 32, :]
    copies = [pltpu.make_async_copy(spread, out_hbm.at[m], sems.at[m]) for m in range(4)]
    for copy in copies:
        copy.start()
    for copy in copies:
        copy.wait()


def spread_rows(weight):
    return pl.pallas_call(
        spread_kernel,
        in_specs=[IN_HBM],
        out_specs=IN_HBM,
        scratch_shapes=[
            pltpu.VMEM((1024, 128), BF16),
            pltpu.VMEM((8, 128, 128), BF16),
            pltpu.SemaphoreType.DMA((5,)),
        ],
        out_shape=jax.ShapeDtypeStruct((4, 8, 128, 128), BF16),
        compiler_params=params(58),
    )(weight)


def gate_kernel(gate_hbm, up_hbm, hidden_hbm, out_ref, *scratch):
    sems = scratch[3]
    copies = []
    for step in range(4):
        rows = pl.ds(step * 256, 256)
        for n, source in enumerate((gate_hbm, up_hbm, hidden_hbm)):
            copy = pltpu.make_async_copy(source.at[rows], scratch[n].at[rows], sems.at[n, step])
            copy.start()
            copies.append(copy)
    for step in range(4):
        rows = pl.ds(step * 256, 256)
        for copy in copies[step * 3 : step * 3 + 3]:
            copy.wait()
        gate, up, hidden = (ref[rows].astype(F32) for ref in scratch[:3])
        sigma = jax.nn.sigmoid(gate)
        product = hidden * up * sigma * (1.0 + gate * (1.0 - sigma))
        out_ref[:, rows] = product.T.astype(BF16)


def gate_gradient(gate_pre, up_value, grad_hidden):
    return pl.pallas_call(
        gate_kernel,
        in_specs=[IN_HBM] * 3,
        out_specs=IN_VMEM,
        scratch_shapes=[pltpu.VMEM((1024, 128), BF16)] * 3 + [pltpu.SemaphoreType.DMA((3, 4))],
        out_shape=jax.ShapeDtypeStruct((128, 1024), BF16),
        compiler_params=params(58),
    )(gate_pre, up_value, grad_hidden)


def share_kernel(gates_ref, tokens_hbm, own_ref, right_ref, left_ref, far_ref, tokens, sems):
    m = lax.axis_index("mp")
    copies = []
    for step in range(8):
        column = jnp.bitwise_and(m + (2, 1, 3, 0)[step // 2], 3) * 1024 + step % 2 * 512
        copy = pltpu.make_async_copy(
            tokens_hbm.at[:, pl.ds(pl.multiple_of(column, 512), 512)], tokens.at[step], sems.at[step]
        )
        copy.start()
        copies.append(copy)
    for step, copy in enumerate(copies):
        copy.wait()
        out_ref = (far_ref, right_ref, left_ref, own_ref)[step // 2]
        share = jnp.dot(gates_ref[...], tokens[step], preferred_element_type=F32)
        out_ref[:, step % 2 * 512 : (step % 2 + 1) * 512] = share.astype(out_ref.dtype)


def weight_shares(gates, tokens):
    return pl.pallas_call(
        share_kernel,
        in_specs=[IN_VMEM, IN_HBM],
        out_specs=[IN_VMEM] * 4,
        scratch_shapes=[pltpu.VMEM((8, 1024, 512), BF16), pltpu.SemaphoreType.DMA((8,))],
        out_shape=[jax.ShapeDtypeStruct((128, 1024), F32)]
        + [jax.ShapeDtypeStruct((128, 1024), BF16)] * 3,
        compiler_params=params(54),
        cost_estimate=pl.CostEstimate(flops=1 << 30, bytes_accessed=10 << 20, transcendentals=0),
    )(gates, tokens)


def join_kernel(own_ref, share_ref, out_ref):
    out_ref[...] = own_ref[...] + share_ref[...].astype(F32)


def join_shares(own, share):
    return pl.pallas_call(
        join_kernel,
        in_specs=[IN_VMEM] * 2,
        out_specs=IN_VMEM,
        out_shape=jax.ShapeDtypeStruct((128, 1024), F32),
        compiler_params=params(),
    )(own, share)


def add_kernel(scale, own_ref, right_ref, far_ref, out_ref):
    total = own_ref[...]
    for ref in (right_ref, far_ref):
        total += ref[...].astype(F32)
    out_ref[...] = (total * scale).T.astype(BF16)


def add_shares(own, away, scale):
    return pl.pallas_call(
        functools.partial(add_kernel, scale),
        in_specs=[IN_VMEM] * 3,
        out_specs=IN_VMEM,
        out_shape=jax.ShapeDtypeStruct((1024, 128), BF16),
        compiler_params=params(),
    )(own, *away)


def partial_kernel(rows_ref, mine_ref, other_ref, out_hbm, rows, total_ref, sems):
    copies = []
    x, c = lax.axis_index("x"), lax.axis_index("c")
    for k in range(8):
        turn = ((0,) + TURNS)[k % 4]
        source = jnp.bitwise_and(x + turn, 3) * 2 + (c if k < 4 else 1 - c)
        for m in range(4):
            rows[m * 128 : (m + 1) * 128, k * 128 : (k + 1) * 128] = rows_ref[m, source]
    for t in range(4):
        columns = pl.ds(t * 256, 256)
        total = jnp.dot(
            rows[:, :512], mine_ref[:, :, columns].reshape(512, 256), preferred_element_type=F32
        )
        total += jnp.dot(
            rows[:, 512:], other_ref[:, :, columns].reshape(512, 256), preferred_element_type=F32
        )
        total_ref[:, columns] = total.astype(BF16)
        copy = pltpu.make_async_copy(total_ref.at[:, columns], out_hbm.at[:, columns], sems.at[t])
        copy.start()
        copies.append(copy)
    for copy in copies:
        copy.wait()


def partial_product(rows, mine, other):
    return pl.pallas_call(
        partial_kernel,
        in_specs=[IN_VMEM] * 3,
        out_specs=IN_HBM,
        scratch_shapes=[
            pltpu.VMEM((512, 1024), BF16),
            pltpu.VMEM((512, 1024), BF16),
            pltpu.SemaphoreType.DMA((4,)),
        ],
        out_shape=jax.ShapeDtypeStruct((512, 1024), BF16),
        compiler_params=params(),
        cost_estimate=pl.CostEstimate(flops=1 << 30, bytes_accessed=4 << 20, transcendentals=0),
    )(rows, mine, other)


def sum_kernel(pieces_ref, out_ref):
    out_ref[...] = jnp.sum(pieces_ref[...].astype(F32), axis=0).astype(BF16)


def sum_pieces(pieces):
    return pl.pallas_call(
        sum_kernel,
        in_specs=[IN_VMEM],
        out_specs=IN_VMEM,
        out_shape=jax.ShapeDtypeStruct((32, 1024), BF16),
        compiler_params=params(),
    )(pieces)


def always(function, *operands):
    shapes = jax.eval_shape(function, *operands)

    def never(*_):
        return jax.tree.map(lambda shape: jnp.zeros(shape.shape, shape.dtype), shapes)

    return lax.cond(lax.axis_index("x") * 2 + lax.axis_index("c") >= 0, function, never, *operands)


def body(tokens, gate_pre, up_value, grad_hidden, gate_weight):
    norm_factor = float(tokens.shape[0] * lax.axis_size("mp")) ** (-0.5)

    rows = spread_rows(gate_weight).reshape(32, 128, 128)
    rows = lax.all_to_all(rows, ("mp", "x", "c"), 0, 0, tiled=True).reshape(4, 8, 128, 128)

    gates = gate_gradient(gate_pre, up_value, grad_hidden)
    mine = [shift(gates, "x", 4, k) for k in TURNS]
    own, *shares = weight_shares(gates, tokens)
    *mine, own = lax.optimization_barrier((*mine, own))
    right, left, far = shares
    right, far = shift(right, "mp", 4, -1), shift(far, "mp", 4, 2)

    def exchange(rows, own, left, *mine):
        mine = jnp.stack(mine)
        partial_sums = partial_product(rows, mine, shift(mine, "c", 2, 1))
        pieces = lax.all_to_all(partial_sums.reshape(16, 32, 1024), ("zl", "y"), 0, 0, tiled=True)
        return sum_pieces(pieces), join_shares(own, shift(left, "mp", 4, 1))

    grad_tokens, own = always(exchange, rows, own, left, gates, *mine)
    grad_tokens, own, right, far = lax.optimization_barrier((grad_tokens, own, right, far))
    return (grad_tokens.T, add_shares(own, (right, far), norm_factor))


def solution(mesh):
    fine = Mesh(mesh.devices.reshape(2, 8, 4, 2, 4), AXES)
    dp = ("zl", "y", "x", "c")
    in_specs = (P("mp", None), P("mp", dp), P("mp", dp), P("mp", dp), P("mp", dp))
    out_specs = (P("mp", dp), P("mp", dp))
    return jax.shard_map(body, mesh=fine, in_specs=in_specs, out_specs=out_specs, check_vma=False)
```

```python
import functools

import jax
import jax.numpy as jnp
from jax import lax
from jax.experimental import pallas as pl
from jax.experimental.pallas import tpu as pltpu
from jax.sharding import Mesh, PartitionSpec as P

TURNS = (2, 1, 3)
AXES = ("zl", "y", "x", "c", "mp")
BF16, F32 = jnp.bfloat16, jnp.float32
IN_HBM = pl.BlockSpec(memory_space=pltpu.HBM)
IN_VMEM = pl.BlockSpec(memory_space=pltpu.VMEM)


def shift(array, axis, size, by):
    return lax.ppermute(array, axis, [((i + by) % size, i) for i in range(size)])


def params(limit=24):
    return pltpu.CompilerParams(vmem_limit_bytes=limit << 20)


def spread_kernel(weight_hbm, out_hbm, weight, spread, sems):
    copy = pltpu.make_async_copy(weight_hbm, weight, sems.at[4])
    copy.start()
    copy.wait()
    for k in range(8):
        for q in range(4):
            spread[k, q * 32 : (q + 1) * 32, :] = weight[(q * 8 + k) * 32 : (q * 8 + k + 1) * 32, :]
    copies = [pltpu.make_async_copy(spread, out_hbm.at[m], sems.at[m]) for m in range(4)]
    for copy in copies:
        copy.start()
    for copy in copies:
        copy.wait()


def spread_rows(weight):
    return pl.pallas_call(
        spread_kernel,
        in_specs=[IN_HBM],
        out_specs=IN_HBM,
        scratch_shapes=[
            pltpu.VMEM((1024, 128), BF16),
            pltpu.VMEM((8, 128, 128), BF16),
            pltpu.SemaphoreType.DMA((5,)),
        ],
        out_shape=jax.ShapeDtypeStruct((4, 8, 128, 128), BF16),
        compiler_params=params(58),
    )(weight)


def gate_kernel(gate_hbm, up_hbm, hidden_hbm, out_ref, *scratch):
    sems = scratch[3]
    copies = []
    for step in range(4):
        rows = pl.ds(step * 256, 256)
        for n, source in enumerate((gate_hbm, up_hbm, hidden_hbm)):
            copy = pltpu.make_async_copy(source.at[rows], scratch[n].at[rows], sems.at[n, step])
            copy.start()
            copies.append(copy)
    for step in range(4):
        rows = pl.ds(step * 256, 256)
        for copy in copies[step * 3 : step * 3 + 3]:
            copy.wait()
        gate, up, hidden = (ref[rows].astype(F32) for ref in scratch[:3])
        sigma = jax.nn.sigmoid(gate)
        product = hidden * up * sigma * (1.0 + gate * (1.0 - sigma))
        out_ref[:, rows] = product.T.astype(BF16)


def gate_gradient(gate_pre, up_value, grad_hidden):
    return pl.pallas_call(
        gate_kernel,
        in_specs=[IN_HBM] * 3,
        out_specs=IN_VMEM,
        scratch_shapes=[pltpu.VMEM((1024, 128), BF16)] * 3 + [pltpu.SemaphoreType.DMA((3, 4))],
        out_shape=jax.ShapeDtypeStruct((128, 1024), BF16),
        compiler_params=params(58),
    )(gate_pre, up_value, grad_hidden)


def share_kernel(gates_ref, tokens_hbm, own_ref, right_ref, left_ref, far_ref, tokens, sems):
    m = lax.axis_index("mp")
    copies = []
    for step in range(8):
        column = jnp.bitwise_and(m + (2, 1, 3, 0)[step // 2], 3) * 1024 + step % 2 * 512
        copy = pltpu.make_async_copy(
            tokens_hbm.at[:, pl.ds(pl.multiple_of(column, 512), 512)], tokens.at[step], sems.at[step]
        )
        copy.start()
        copies.append(copy)
    for step, copy in enumerate(copies):
        copy.wait()
        out_ref = (far_ref, right_ref, left_ref, own_ref)[step // 2]
        share = jnp.dot(gates_ref[...], tokens[step], preferred_element_type=F32)
        out_ref[:, step % 2 * 512 : (step % 2 + 1) * 512] = share.astype(out_ref.dtype)


def weight_shares(gates, tokens):
    return pl.pallas_call(
        share_kernel,
        in_specs=[IN_VMEM, IN_HBM],
        out_specs=[IN_VMEM] * 4,
        scratch_shapes=[pltpu.VMEM((8, 1024, 512), BF16), pltpu.SemaphoreType.DMA((8,))],
        out_shape=[jax.ShapeDtypeStruct((128, 1024), F32)]
        + [jax.ShapeDtypeStruct((128, 1024), BF16)] * 3,
        compiler_params=params(54),
        cost_estimate=pl.CostEstimate(flops=1 << 30, bytes_accessed=10 << 20, transcendentals=0),
    )(gates, tokens)


def add_kernel(scale, own_ref, right_ref, left_ref, far_ref, out_ref):
    total = own_ref[...]
    for ref in (right_ref, left_ref, far_ref):
        total += ref[...].astype(F32)
    out_ref[...] = (total * scale).T.astype(BF16)


def add_shares(own, away, scale):
    return pl.pallas_call(
        functools.partial(add_kernel, scale),
        in_specs=[IN_VMEM] * 4,
        out_specs=IN_VMEM,
        out_shape=jax.ShapeDtypeStruct((1024, 128), BF16),
        compiler_params=params(),
    )(own, *away)


def partial_kernel(rows_ref, mine_ref, other_ref, out_ref, rows):
    x, c = lax.axis_index("x"), lax.axis_index("c")
    for k in range(8):
        turn = ((0,) + TURNS)[k % 4]
        source = jnp.bitwise_and(x + turn, 3) * 2 + (c if k < 4 else 1 - c)
        for m in range(4):
            rows[m * 128 : (m + 1) * 128, k * 128 : (k + 1) * 128] = rows_ref[m, source]
    for t in range(2):
        columns = pl.ds(t * 512, 512)
        total = jnp.dot(
            rows[:, :512], mine_ref[:, :, columns].reshape(512, 512), preferred_element_type=F32
        )
        total += jnp.dot(
            rows[:, 512:], other_ref[:, :, columns].reshape(512, 512), preferred_element_type=F32
        )
        out_ref[:, columns] = total.astype(BF16)


def partial_product(rows, mine, other):
    return pl.pallas_call(
        partial_kernel,
        in_specs=[IN_VMEM] * 3,
        out_specs=IN_VMEM,
        scratch_shapes=[pltpu.VMEM((512, 1024), BF16)],
        out_shape=jax.ShapeDtypeStruct((512, 1024), BF16),
        compiler_params=params(),
        cost_estimate=pl.CostEstimate(flops=1 << 30, bytes_accessed=4 << 20, transcendentals=0),
    )(rows, mine, other)


def sum_kernel(pieces_ref, out_ref):
    out_ref[...] = jnp.sum(pieces_ref[...].astype(F32), axis=0).astype(BF16)


def sum_pieces(pieces):
    return pl.pallas_call(
        sum_kernel,
        in_specs=[IN_VMEM],
        out_specs=IN_VMEM,
        out_shape=jax.ShapeDtypeStruct((32, 1024), BF16),
        compiler_params=params(),
    )(pieces)


def always(function, *operands):
    shapes = jax.eval_shape(function, *operands)

    def never(*_):
        return jax.tree.map(lambda shape: jnp.zeros(shape.shape, shape.dtype), shapes)

    return lax.cond(lax.axis_index("x") * 2 + lax.axis_index("c") >= 0, function, never, *operands)


def body(tokens, gate_pre, up_value, grad_hidden, gate_weight):
    norm_factor = float(tokens.shape[0] * lax.axis_size("mp")) ** (-0.5)

    rows = spread_rows(gate_weight).reshape(32, 128, 128)
    rows = lax.all_to_all(rows, ("mp", "x", "c"), 0, 0, tiled=True).reshape(4, 8, 128, 128)

    gates = gate_gradient(gate_pre, up_value, grad_hidden)
    mine = [shift(gates, "x", 4, k) for k in TURNS]
    own, *shares = weight_shares(gates, tokens)
    *mine, own = lax.optimization_barrier((*mine, own))
    right, left, far = shares
    right, far = shift(right, "mp", 4, -1), shift(far, "mp", 4, 2)

    def exchange(rows, left, *mine):
        mine = jnp.stack(mine)
        partial_sums = partial_product(rows, mine, shift(mine, "c", 2, 1))
        pieces = lax.all_to_all(partial_sums.reshape(16, 32, 1024), ("zl", "y"), 0, 0, tiled=True)
        return sum_pieces(pieces), shift(left, "mp", 4, 1)

    grad_tokens, left = always(exchange, rows, left, gates, *mine)
    grad_tokens, own, right, left, far = lax.optimization_barrier((grad_tokens, own, right, left, far))
    return (grad_tokens.T, add_shares(own, (right, left, far), norm_factor))


def solution(mesh):
    fine = Mesh(mesh.devices.reshape(2, 8, 4, 2, 4), AXES)
    dp = ("zl", "y", "x", "c")
    in_specs = (P("mp", None), P("mp", dp), P("mp", dp), P("mp", dp), P("mp", dp))
    out_specs = (P("mp", dp), P("mp", dp))
    return jax.shard_map(body, mesh=fine, in_specs=in_specs, out_specs=out_specs, check_vma=False)
```
